32 devices in a mesh: section: 2 (over core), dp: 16 (over z, y, x).
Axes of the slice: x: 2, y: 2, z: 4, core: 2. Of those that a mesh axis runs over, the one named last changes fastest.
Arguments:
- embeddings: bfloat16 [2, 16384, 512], P('section', 'dp'), may hold values from -6 to 6
- cotangent: bfloat16 [16384, 512], P('dp'), may hold values from -6 to 6
- source_lengths: int32 [32, 8], P('dp'), may hold values from 1 to 256, 512 in all within a row
- target_lengths: int32 [32, 8], P('dp'), may hold values from 1 to 256, 512 in all within a row
- self_routes: int32 [2, 16384, 2], P('section', 'dp'), may hold values from 0 to 7, all different within a row
- cross_routes: int32 [16384, 2], P('dp'), may hold values from 0 to 7, all different within a row
- attend_gain: float32 [2, 512], P('section'), may hold values from 0.5 to 1.5
- attend_bias: float32 [2, 512], P('section'), may hold values from -1.25 to 1.25
- self_router: bfloat16 [2, 512, 8], P('section'), may hold values from -0.1875 to 0.1875
- query_weight: bfloat16 [2, 512, 512], P('section'), may hold values from -0.25 to 0.25
- key_weight: bfloat16 [2, 512, 64], P('section'), may hold values from -0.25 to 0.25
- value_weight: bfloat16 [2, 512, 64], P('section'), may hold values from -0.25 to 0.25
- output_weight: bfloat16 [2, 512, 512], P('section'), may hold values from -4 to 4
- feed_gain: float32 [2, 512], P('section'), may hold values from 0.5 to 1.5
- feed_bias: float32 [2, 512], P('section'), may hold values from -1.25 to 1.25
- expand_weight: bfloat16 [2, 512, 2048], P('section'), may hold values from -0.25 to 0.25
- expand_bias: float32 [2, 2048], P('section'), may hold values from -1.75 to 1.75
- reduce_weight: bfloat16 [2, 2048, 512], P('section'), may hold values from -0.125 to 0.125
- reduce_bias: float32 [2, 512], P('section'), may hold values from -1.75 to 1.75
- cross_gain: float32 [512], replicated, may hold values from 0.5 to 1.5
- cross_bias: float32 [512], replicated, may hold values from -1.25 to 1.25
- cross_router: bfloat16 [512, 8], replicated, may hold values from -0.1875 to 0.1875
- cross_query: bfloat16 [512, 512], replicated, may hold values from -0.25 to 0.25
- cross_key: bfloat16 [512, 64], replicated, may hold values from -0.25 to 0.25
- cross_value: bfloat16 [512, 64], replicated, may hold values from -0.25 to 0.25
- cross_output: bfloat16 [512, 512], replicated, may hold values from -4 to 4
Outputs:
- activations: bfloat16 [2, 16384, 512], P('section', 'dp')
- input_grads: float32 [2, 16384, 512], P('section', 'dp')
- grad_attend_gain: float32 [2, 512], P('section')
- grad_attend_bias: float32 [2, 512], P('section')
- grad_self_router: float32 [2, 512, 8], P('section')
- grad_query_weight: float32 [2, 512, 512], P('section')
- grad_key_weight: float32 [2, 512, 64], P('section')
- grad_value_weight: float32 [2, 512, 64], P('section')
- grad_output_weight: float32 [2, 512, 512], P('section')
- grad_feed_gain: float32 [2, 512], P('section')
- grad_feed_bias: float32 [2, 512], P('section')
- grad_expand_weight: float32 [2, 512, 2048], P('section')
- grad_expand_bias: float32 [2, 2048], P('section')
- grad_reduce_weight: float32 [2, 2048, 512], P('section')
- grad_reduce_bias: float32 [2, 512], P('section')
- grad_cross_gain: float32 [512], replicated
- grad_cross_bias: float32 [512], replicated
- grad_cross_router: float32 [512, 8], replicated
- grad_cross_query: float32 [512, 512], replicated
- grad_cross_key: float32 [512, 64], replicated
- grad_cross_value: float32 [512, 64], replicated
- grad_cross_output: float32 [512, 512], replicated
The draws below stay inside these ranges and needn't reach their ends.
Inputs may be any that keep to these rules, and one draw needn't show every extreme that they name: `source_lengths`: each row of 8 sentence lengths sums to 512, and its longest sentence has exactly 256 tokens. `target_lengths`: each row of 8 sentence lengths sums to 512, and its longest sentence has exactly 256 tokens. `self_routes`: each token names 2 different experts. `cross_routes`: each token names 2 different experts.
All inputs are finite; a program needn't handle non-finite values.
Results may differ from the reference program's by a relative error of at most 0.022.
The reference program's roundings to bfloat16 on the way count: a program that leaves them out, or rounds other values in their place, can miss the bound.
Values may be sent and summed in bfloat16 or wider, within the bound.
A program may use at most 192 MiB of HBM per device.

```python
import math
import jax
import jax.numpy as jnp
import numpy as np
from jax import lax

D = 512
HEADS = 8
HEAD_DIM = 64
FF = 2048
TOPK = 2
SLOT = 512
SENTS = 8
MOST = 256
SLOTS = 32
ROWS = 16384


def block_levels(key, shape, shards, smallest, high):
    factor_of, own = 1.0, jax.random.fold_in(key, 6)
    for axis_at, parts in shards:
        draws = jnp.exp(jax.random.uniform(jax.random.fold_in(own, axis_at), (parts,), jnp.float32, smallest / len(shards), high / len(shards)))
        factor_of = factor_of * jnp.repeat(draws, shape[axis_at] // parts).reshape([-1 if axis == axis_at else 1 for axis in range(len(shape))])
    return factor_of


def different_ones(own_key, rows, amount, top, lift):
    sequence = jax.random.permutation(jax.random.fold_in(own_key, 1), amount)
    pull = sequence
    for power in range(3):
        pull = pull * pull // amount
    pull = pull * lift // amount
    tickets = jax.random.randint(jax.random.fold_in(own_key, 2), (rows, amount), 0, 4096) + pull
    sure = jax.random.permutation(jax.random.fold_in(own_key, 3), rows)[jnp.arange(amount) % rows]
    tickets = jnp.where(jnp.arange(rows)[:, None] == sure[None, :], 1 << 14, tickets)
    merit = tickets * amount + jnp.arange(amount)
    return lax.top_k(merit.astype(jnp.int32), top)[1].astype(jnp.int32)


def profile(count, total, bound, lean):
    portions = [(1 << 20) // math.isqrt(grade ** lean) + 1 for grade in range(2, count + 1)]
    surplus, holding = total - bound - (count - 1), [1] * (count - 1)
    while surplus > 0:
        movable = [i for i in range(count - 1) if holding[i] < bound]
        whole, budget = sum([portions[i] for i in movable]), surplus
        for i in movable:
            more = min(bound - holding[i], max(1, budget * portions[i] // whole), surplus)
            holding[i] = holding[i] + more
            surplus = surplus - more
    return np.array([bound] + holding)


def uneven(rng, count, total, bound, skew):
    if count == 2:
        one = jax.random.randint(rng, (), max(1, total - bound), min(bound, total - 1) + 1)
        return jnp.stack([one, total - one])
    sizes = jnp.asarray(profile(count, total, bound, skew), jnp.int32)
    couples = (count - 1) // 2
    source_of, taker = sizes[1:1 + 2 * couples:2], sizes[2:2 + 2 * couples:2]
    room = jnp.minimum(source_of - 1, bound - taker)
    passed = jax.random.randint(jax.random.fold_in(rng, 1), (couples,), 0, 1 << 20) % (room + 1)
    sizes = sizes.at[1:1 + 2 * couples:2].set(source_of - passed).at[2:2 + 2 * couples:2].set(taker + passed)
    return sizes[jax.random.permutation(jax.random.fold_in(rng, 2), count)]


def gaussian(key, shape, scale, most, shards=(), kind=jnp.bfloat16):
    factor_of = block_levels(key, shape, shards, -0.22, 0.18) if shards else 1.0
    result = jax.random.normal(key, shape, jnp.float32) * scale * factor_of
    return jnp.minimum(jnp.maximum(result, -most), most).astype(kind)


def setup_inputs(seed: int = 0) -> dict:
    streams_of = jax.random.split(jax.random.key(seed), 27)
    return {
        "embeddings": gaussian(streams_of[0], (2, ROWS, D), 1.0, 6.0, ((0, 2), (1, 16))),
        "cotangent": gaussian(streams_of[1], (ROWS, D), 1.0, 6.0, ((0, 16),)),
        "source_lengths": jax.vmap(lambda own: uneven(own, SENTS, SLOT, MOST, 2))(jax.random.split(streams_of[2], SLOTS)).reshape((SLOTS, SENTS)).astype(jnp.int32),
        "target_lengths": jax.vmap(lambda own: uneven(own, SENTS, SLOT, MOST, 2))(jax.random.split(streams_of[3], SLOTS)).reshape((SLOTS, SENTS)).astype(jnp.int32),
        "self_routes": different_ones(streams_of[4], 2 * ROWS, HEADS, TOPK, 2048).reshape((2, ROWS, TOPK)),
        "cross_routes": different_ones(streams_of[5], ROWS, HEADS, TOPK, 2048),
        "attend_gain": jnp.clip(1.0 + 0.1 * jax.random.normal(streams_of[6], (2, D), jnp.float32), 0.5, 1.5),
        "attend_bias": gaussian(streams_of[7], (2, D), 0.2, 1.25, ((0, 2),), jnp.float32),
        "self_router": gaussian(streams_of[8], (2, D, HEADS), 0.03, 0.1875, ((0, 2),)),
        "query_weight": gaussian(streams_of[9], (2, D, HEADS * HEAD_DIM), D ** -0.5, 0.25, ((0, 2),)),
        "key_weight": gaussian(streams_of[10], (2, D, HEAD_DIM), D ** -0.5, 0.25, ((0, 2),)),
        "value_weight": gaussian(streams_of[11], (2, D, HEAD_DIM), D ** -0.5, 0.25, ((0, 2),)),
        "output_weight": gaussian(streams_of[12], (2, HEADS * HEAD_DIM, D), 2 ** -0.5, 4.0, ((0, 2),)),
        "feed_gain": jnp.clip(1.0 + 0.1 * jax.random.normal(streams_of[13], (2, D), jnp.float32), 0.5, 1.5),
        "feed_bias": gaussian(streams_of[14], (2, D), 0.2, 1.25, ((0, 2),), jnp.float32),
        "expand_weight": gaussian(streams_of[15], (2, D, FF), D ** -0.5, 0.25, ((0, 2),)),
        "expand_bias": gaussian(streams_of[16], (2, FF), 0.3, 1.75, ((0, 2),), jnp.float32),
        "reduce_weight": gaussian(streams_of[17], (2, FF, D), FF ** -0.5, 0.125, ((0, 2),)),
        "reduce_bias": gaussian(streams_of[18], (2, D), 0.3, 1.75, ((0, 2),), jnp.float32),
        "cross_gain": jnp.clip(1.0 + 0.1 * jax.random.normal(streams_of[19], (D,), jnp.float32), 0.5, 1.5),
        "cross_bias": gaussian(streams_of[20], (D,), 0.2, 1.25, (), jnp.float32),
        "cross_router": gaussian(streams_of[21], (D, HEADS), 0.03, 0.1875),
        "cross_query": gaussian(streams_of[22], (D, HEADS * HEAD_DIM), D ** -0.5, 0.25),
        "cross_key": gaussian(streams_of[23], (D, HEAD_DIM), D ** -0.5, 0.25),
        "cross_value": gaussian(streams_of[24], (D, HEAD_DIM), D ** -0.5, 0.25),
        "cross_output": gaussian(streams_of[25], (HEADS * HEAD_DIM, D), 2 ** -0.5, 4.0),
    }


EPSILON = 1e-05
SCORE_SCALE = 0.125
MASKED_SCORE = -1000000000.0
HIGHEST = lax.Precision.HIGHEST

@jax.custom_vjp
def low(v):
    return lax.optimization_barrier(v.astype(jnp.bfloat16)).astype(jnp.float32)

@jax.custom_vjp
def low_back(v):
    return v

def low_keep(v):
    return (low(v), None)

def low_pass(kept, grad):
    return (grad,)

def back_keep(v):
    return (v, None)

def back_low(kept, grad):
    return (low(grad),)
low.defvjp(low_keep, low_pass)
low_back.defvjp(back_keep, back_low)

def both_ways(value):
    return low(low_back(value))

def layer_norm(values, norm_gain, norm_shift):
    average = lax.optimization_barrier(jnp.mean(values, axis=-1, keepdims=True))
    centred = values - average
    spread = lax.optimization_barrier(jnp.mean(centred * centred, axis=-1, keepdims=True))
    return centred * lax.rsqrt(spread + EPSILON) * norm_gain + norm_shift

def segment_ids(lengths, slot_rows):
    boundary = jnp.cumsum(lengths)
    places = lax.iota(jnp.int32, slot_rows)
    return lax.optimization_barrier(jnp.sum((places[:, None] >= boundary[None, :]).astype(jnp.int32), axis=1))

def pick_gates(logits, routes):
    experts = logits.shape[-1]
    chosen = lax.optimization_barrier(jnp.sum((routes[..., :, None] == lax.iota(jnp.int32, experts)).astype(logits.dtype), axis=-2))
    scaled = chosen * jnp.exp(logits)
    return scaled / lax.optimization_barrier(jnp.sum(scaled, axis=-1, keepdims=True))

def slot_attention(queries, key_rows, value_rows, query_ids, key_ids, causal):
    slot_rows = query_ids.shape[0]
    allowed = query_ids[:, None] == key_ids[None, :]
    if causal:
        places = lax.iota(jnp.int32, slot_rows)
        allowed = allowed & (places[:, None] >= places[None, :])
    raw_scores = jnp.einsum('thd,sd->hts', queries, key_rows, precision=HIGHEST)
    scores = jnp.where(allowed[None], low_back(raw_scores * SCORE_SCALE), MASKED_SCORE)
    chance = low(jax.nn.softmax(scores, axis=-1))
    return low_back(jnp.einsum('hts,sd->thd', chance, value_rows, precision=HIGHEST))

def mixture(normed, source, routes, weights, query_ids, key_ids, causal):
    router, query_weight, key_weight, value_weight, output_weight = weights
    slot_count = normed.shape[0]
    slot_rows = normed.shape[1]
    head_count = router.shape[1]
    logits = jnp.einsum('ntd,de->nte', normed, router, precision=HIGHEST)
    gate_values = pick_gates(logits, routes)
    queries = both_ways(jnp.einsum('ntd,dk->ntk', normed, query_weight, precision=HIGHEST))
    queries = queries.reshape(slot_count, slot_rows, head_count, -1)
    key_rows = both_ways(jnp.einsum('ntd,dk->ntk', source, key_weight, precision=HIGHEST))
    value_rows = both_ways(jnp.einsum('ntd,dk->ntk', source, value_weight, precision=HIGHEST))

    def one_slot(pieces):
        return slot_attention(pieces[0], pieces[1], pieces[2], pieces[3], pieces[4], causal)
    blended = lax.map(jax.checkpoint(one_slot), (queries, key_rows, value_rows, query_ids, key_ids))
    gated_heads = both_ways(gate_values[..., None] * blended).reshape(slot_count, slot_rows, -1)
    return low_back(jnp.einsum('ntk,kd->ntd', gated_heads, output_weight, precision=HIGHEST))

def feed_forward(normed, weights):
    expand_weight, expand_bias, reduce_weight, reduce_bias = weights
    pre_active = low_back(jnp.einsum('ntd,df->ntf', normed, expand_weight, precision=HIGHEST) + expand_bias)
    hidden = low(jax.nn.gelu(pre_active))
    return low_back(jnp.einsum('ntf,fd->ntd', hidden, reduce_weight, precision=HIGHEST) + reduce_bias)

def run_layer(residual, stacked, routes, own_ids, causal, cross_parts):
    normed = low(layer_norm(residual, stacked[0], stacked[1]))
    residual = residual + mixture(normed, normed, routes, stacked[2:7], own_ids, own_ids, causal)
    if cross_parts is not None:
        memory_low, cross_weights, cross_choice, source_ids = cross_parts
        normed = low(layer_norm(residual, cross_weights[0], cross_weights[1]))
        residual = residual + mixture(normed, memory_low, cross_choice, cross_weights[2:7], own_ids, source_ids, False)
    normed = low(layer_norm(residual, stacked[7], stacked[8]))
    return residual + feed_forward(normed, stacked[9:13])

def reference(embeddings, cotangent, source_lengths, target_lengths, self_routes, cross_routes, attend_gain, attend_bias, self_router, query_weight, key_weight, value_weight, output_weight, feed_gain, feed_bias, expand_weight, expand_bias, reduce_weight, reduce_bias, cross_gain, cross_bias, cross_router, cross_query, cross_key, cross_value, cross_output):
    slot_count = source_lengths.shape[0]
    slot_rows = embeddings.shape[1] // slot_count
    model_width = embeddings.shape[2]
    source_ids = jax.vmap(lambda lengths: segment_ids(lengths, slot_rows))(source_lengths)
    target_ids = jax.vmap(lambda lengths: segment_ids(lengths, slot_rows))(target_lengths)
    stacked = tuple((weight.astype(jnp.float32) for weight in (attend_gain, attend_bias, self_router, query_weight, key_weight, value_weight, output_weight, feed_gain, feed_bias, expand_weight, expand_bias, reduce_weight, reduce_bias)))
    cross_weights = tuple((weight.astype(jnp.float32) for weight in (cross_gain, cross_bias, cross_router, cross_query, cross_key, cross_value, cross_output)))
    inputs = embeddings.astype(jnp.float32).reshape(2, slot_count, slot_rows, model_width)
    routes = self_routes.reshape(2, slot_count, slot_rows, -1)
    cross_choice = cross_routes.reshape(slot_count, slot_rows, -1)

    def forward(stacked_weights, cross_part_weights, layer_inputs):
        encoder_weights = tuple((weight[0] for weight in stacked_weights))
        decoder_weights = tuple((weight[1] for weight in stacked_weights))
        memory = run_layer(layer_inputs[0], encoder_weights, routes[0], source_ids, False, None)
        memory_low = low(low_back(memory))
        output = run_layer(layer_inputs[1], decoder_weights, routes[1], target_ids, True, (memory_low, cross_part_weights, cross_choice, source_ids))
        return (output, memory)
    output, backward, memory = jax.vjp(forward, stacked, cross_weights, inputs, has_aux=True)
    stack_grads, cross_grads, input_grads = backward(cotangent.astype(jnp.float32).reshape(slot_count, slot_rows, model_width))
    activations = jnp.stack([memory, output]).astype(jnp.bfloat16).reshape(2, -1, model_width)
    input_grads = input_grads.reshape(2, -1, model_width)
    return (activations, input_grads, stack_grads[0], stack_grads[1], stack_grads[2], stack_grads[3], stack_grads[4], stack_grads[5], stack_grads[6], stack_grads[7], stack_grads[8], stack_grads[9], stack_grads[10], stack_grads[11], stack_grads[12], cross_grads[0], cross_grads[1], cross_grads[2], cross_grads[3], cross_grads[4], cross_grads[5], cross_grads[6])
```

```python
import functools
import math

import jax
import jax.numpy as jnp
from jax import lax
from jax.experimental import pallas as pl
from jax.experimental.pallas import tpu as pltpu
from jax.sharding import PartitionSpec as P

EPSILON = 1e-05
SCORE_SCALE = 0.125
MASKED_SCORE = -1000000000.0
F32 = jnp.float32
BF16 = jnp.bfloat16
T = 512
D = 512
FF = 2048
PAIR = 128
CH = 512
PARTS = 2
PART = FF // PARTS
NARROW = 160
MESH = pl.DeviceIdType.MESH


def dot(a, b):
    return lax.dot_general(a, b, (((1,), (0,)), ((), ())), preferred_element_type=F32)


def dot_nt(a, b):
    return lax.dot_general(a, b, (((1,), (1,)), ((), ())), preferred_element_type=F32)


def dot_tn(a, b):
    return lax.dot_general(a, b, (((0,), (0,)), ((), ())), preferred_element_type=F32)


def iota(shape, axis):
    return lax.broadcasted_iota(jnp.int32, shape, axis)


def norm_parts(v):
    centred = v - jnp.mean(v, axis=-1, keepdims=True)
    spread = jnp.mean(centred * centred, axis=-1, keepdims=True)
    return centred, lax.rsqrt(spread + EPSILON)


def norm(v, gain, bias):
    centred, scale = norm_parts(v)
    return centred * scale * gain + bias


def norm_back(dn, v, gain):
    centred, scale = norm_parts(v)
    unit = centred * scale
    dgain = jnp.sum(dn * unit, axis=0, keepdims=True)
    dbias = jnp.sum(dn, axis=0, keepdims=True)
    dunit = dn * gain
    first = jnp.mean(dunit, axis=-1, keepdims=True)
    second = jnp.mean(dunit * unit, axis=-1, keepdims=True)
    return scale * (dunit - first - unit * second), dgain, dbias


def ids_of(ends, shape, axis):
    places = iota(shape, axis)
    total = jnp.zeros(shape, jnp.int32)
    for end in ends:
        total = total + (places >= end).astype(jnp.int32)
    return total


def ends_of(lengths):
    ends, total = [], jnp.int32(0)
    for length in lengths:
        total = total + length
        ends.append(total)
    return ends


def same_of(key_ends, query_ends):
    return ids_of(key_ends, (T, 1), 0) == ids_of(query_ends, (1, T), 1)


def earlier():
    return iota((T, T), 0) <= iota((T, T), 1)


def chosen(expert, block):
    return expert == (iota((T, PAIR), 1) // 64 + 2 * block).astype(F32)


def laid_out(row):
    return jnp.broadcast_to(row, (PAIR, T)).T


def mixture_fwd(a, s, experts, w, allowed, kept, with_out=True):
    wq, wk2, wv2, wkv, wr2, wo = w
    q = dot(a, wq[...])
    logits = dot_nt(a, wr2[...])
    kk = dot_nt(s, wk2[...]).astype(BF16)
    vv = dot_nt(s, wv2[...]).astype(BF16)
    kept["kk"][...] = kk
    kept["vv"][...] = vv
    lanes = iota((T, PAIR), 1).astype(F32)
    raised = [
        jnp.exp(jnp.sum(jnp.where(lanes == e, logits, 0.0), axis=-1, keepdims=True))
        for e in experts
    ]
    total = raised[0] + raised[1]
    gated = [jnp.zeros((T, PAIR), F32) for _ in range(4)]
    for r in range(2):
        gate = raised[r] / total
        kept["gate"][r] = jnp.broadcast_to(gate, (T, PAIR))
        qs = jnp.zeros((T, PAIR), F32)
        for b in range(4):
            qs = jnp.where(chosen(experts[r], b), q[:, b * PAIR : (b + 1) * PAIR], qs)
        qs = qs.astype(BF16)
        kept["qs"][r] = qs
        scores = jnp.where(allowed, dot_nt(kk, qs) * SCORE_SCALE, MASKED_SCORE)
        top = jnp.max(scores, axis=0, keepdims=True)
        p = jnp.exp(scores - top)
        inverse = 1.0 / jnp.sum(p, axis=0, keepdims=True)
        kept["top"][r : r + 1] = top
        kept["inv"][r : r + 1] = inverse
        chance = (p * inverse).astype(BF16)
        mixed = dot_tn(vv, chance).T
        kept["mixed"][r] = mixed
        weighted = gate * mixed
        for b in range(4):
            gated[b] = jnp.where(chosen(experts[r], b), weighted, gated[b])
    for b in range(4):
        kept["gated"][:, b * PAIR : (b + 1) * PAIR] = gated[b].astype(BF16)
    if with_out:
        return dot(kept["gated"][...], wo[...])


def mixture_bwd(dy, a, s, experts, w, allowed, kept, wide, base, narrow, nbase, mark):
    wq, wk2, wv2, wkv, wr2, wo = w
    wide[base + D : base + 2 * D, :] = dot_tn(kept["gated"][...], dy).astype(BF16)
    dgated = dot_nt(dy, wo[...]).astype(BF16).astype(F32)
    kk, vv = kept["kk"][...], kept["vv"][...]
    lanes = iota((T, PAIR), 1)
    dkk = jnp.zeros((T, PAIR), F32)
    dvv = jnp.zeros((T, PAIR), F32)
    dgates, gates, dqs = [], [], []
    for r in range(2):
        own = jnp.zeros((T, PAIR), F32)
        for b in range(4):
            own = jnp.where(chosen(experts[r], b), dgated[:, b * PAIR : (b + 1) * PAIR], own)
        gate = kept["gate"][r]
        gates.append(gate)
        dgates.append(jnp.sum(own * kept["mixed"][r], axis=-1, keepdims=True))
        dmixed = (gate * own).astype(BF16)
        qs = kept["qs"][r]
        scores = jnp.where(allowed, dot_nt(kk, qs) * SCORE_SCALE, MASKED_SCORE)
        p = jnp.exp(scores - kept["top"][r : r + 1]) * kept["inv"][r : r + 1]
        dp = dot_nt(vv, dmixed)
        both = jnp.sum(p * dp, axis=0, keepdims=True)
        ds = (p * (dp - both)).astype(BF16)
        dkk = dkk + dot(ds, qs)
        dvv = dvv + dot(p.astype(BF16), dmixed)
        dqs.append((dot_tn(kk, ds) * SCORE_SCALE).T)
        mark()
    dq = []
    for b in range(4):
        part = jnp.zeros((T, PAIR), F32)
        for r in range(2):
            part = jnp.where(chosen(experts[r], b), dqs[r], part)
        dq.append(part.astype(BF16))
    dq = jnp.concatenate(dq, axis=1)
    dk = (dkk + pltpu.roll(dkk, 64, 1)) * SCORE_SCALE
    dv = dvv + pltpu.roll(dvv, 64, 1)
    dkv = jnp.where(lanes < 64, dk, dv).astype(BF16)
    mean = gates[0] * dgates[0] + gates[1] * dgates[1]
    dl = jnp.zeros((T, PAIR), F32)
    for r in range(2):
        dl = jnp.where(((lanes % 8).astype(F32) == experts[r]) & (lanes < 16), gates[r] * (dgates[r] - mean), dl)
    high = dl.astype(BF16).astype(F32)
    dl = jnp.where(lanes < 8, high, dl - high).astype(BF16)
    wide[base : base + D, :] = dot_tn(a, dq).astype(BF16)
    narrow[nbase : nbase + PAIR, :] = dot_tn(dkv, s).astype(BF16)
    dwr = dot_tn(dl, a)
    dwr = dwr[0:8] + dwr[8:16]
    narrow[nbase + PAIR : nbase + PAIR + 16, :] = jnp.concatenate([dwr, jnp.zeros((8, D), F32)], axis=0).astype(BF16)
    da = dot_nt(dq, wq[...]) + dot(dl, wr2[...])
    ds = dot(dkv, wkv[...])
    return da, ds


C0, C1 = 0.7978845608028654, 0.044715


def gelu(pre):
    half = 0.5 * jnp.tanh(C0 * (pre + C1 * pre * pre * pre)) + 0.5
    return pre * half


def gelu_both(pre):
    square = pre * pre
    t = jnp.tanh(C0 * pre * (1.0 + C1 * square))
    half = 0.5 * t + 0.5
    slope = half + 0.5 * pre * (1.0 - t * t) * (C0 * (1.0 + 3.0 * C1 * square))
    return pre * half, slope


def expand_step(j, f, we, p):
    at = pl.multiple_of(j * CH, CH)
    return dot(f[...], we[:, pl.ds(at, CH)]) + p[pl.ds(5 + j, 1), :]


def feed_fwd(pairs, we, p, wr):
    def step(j, carry):
        at = pl.multiple_of(j * CH, CH)
        for f, acc in pairs:
            hidden = gelu(expand_step(j, f, we, p)).astype(BF16)
            acc[...] += dot(hidden, wr[pl.ds(at, CH), :])
        return carry

    lax.fori_loop(0, FF // CH, step, 0)


def feed_both(part, f, ft, dy_ref, we, p, wr, acc, dacc, g, deb):
    def step(i, carry):
        j = part * (PART // CH) + i
        at = pl.multiple_of(j * CH, CH)
        to = pl.multiple_of(i * CH, CH)
        dy = dy_ref[...]
        hidden, slope = gelu_both(expand_step(j, f, we, p))
        hidden = hidden.astype(BF16)
        if acc is not None:
            acc[...] += dot(hidden, wr[pl.ds(at, CH), :])
        g[pl.ds(pl.multiple_of(PART + to, CH), CH), :] = dot_tn(hidden, dy).astype(BF16)
        dpre = (dot_nt(dy, wr[pl.ds(at, CH), :]) * slope).astype(BF16)
        deb[pl.ds(j, 1), :] = jnp.sum(dpre.astype(F32), axis=0, keepdims=True)
        g[pl.ds(to, CH), :] = dot(ft[...], dpre).astype(BF16)
        dacc[...] += dot_nt(dpre, we[:, pl.ds(at, CH)])
        return carry

    lax.fori_loop(0, PART // CH, step, 0)


def small_rows(rows, count=16):
    places = iota((count, D), 0)
    out = jnp.zeros((count, D), F32)
    for i, row in enumerate(rows):
        out = jnp.where(places == i, row, out)
    return out


KEPT = (
    ("kk", (T, PAIR), BF16),
    ("vv", (T, PAIR), BF16),
    ("gate", (2, T, PAIR), F32),
    ("qs", (2, T, PAIR), BF16),
    ("top", (8, T), F32),
    ("inv", (8, T), F32),
    ("mixed", (2, T, PAIR), F32),
    ("gated", (T, D), BF16),
)


class Here:
    def __init__(self, n):
        self.bits = n.bit_length() - 1
        self.sec = lax.axis_index("section")
        self.rank = lax.axis_index("dp")

    def side(self, b):
        return lax.rem(self.rank // (1 << b), 2)

    def partner(self, b):
        return (self.sec, self.rank + (1 - 2 * self.side(b)) * (1 << b))

    def twin(self):
        return (1 - self.sec, self.rank)


def scattered(n):
    return min(4, n.bit_length() - 1)


def up(rows, n):
    unit = 16 << scattered(n)
    return -(-rows // unit) * unit


PLAN = (
    ((1, (0, 2, 1, 3)), (2, (0, 1, 2, 3)), (1, (1, 0, 3, 2))),
    ((1, (1, 0, 2, 3)), (2, (0, 1, 2, 3)), (1, (1, 0, 3, 2))),
    ((1, (0, 1, 3, 2)), (1, (1, 0, 3, 2))),
    ((2, (0, 1, 2, 3)), (1, (0, 1, 2, 3)), (1, (2, 0, 1, 3))),
    ((1, (2, 1, 3, 0)), (2, (0, 1, 2, 3)), (1, (1, 2, 0, 3))),
    ((1, (1, 2, 0, 3)), (1, (1, 3, 2, 0))),
    ((1, (1, 0, 2, 3)), (1, (0, 1, 2, 3)), (1, (1, 2, 0, 3))),
)
MARKS = (
    (),
    (3, 4, 5, 0),
    (2,),
    (),
    (0, 3, 1, 6, 7, 5),
    (0, 4, 1, 2, 3, 7),
    (0, 6, 1, 5, 4, 2, 3, 7, 11, 12, 13),
    (10, 6, 0),
    (1, 8, 4, 2, 5, 3, 13, 9, 0),
    (7, 11),
    (2, 8, 5, 6, 14, 15, 9, 1, 12, 11, 4, 13, 10, 3, 0, 7),
    (2, 8, 13, 5, 14, 6, 9),
    (1, 0, 15),
    (3, 11, 2, 7, 4, 0, 12, 10, 8, 13, 14, 16, 17, 6, 18, 5, 1, 3, 9, 11),
    (
        14, 4, 2, 15, 7, 17, 12, 2, 16, 10, 5, 15, 8, 13, 18, 6, 9, 14, 3, 1, 8, 12, 11, 10,
        3, 7, 18, 4, 1, 9, 16, 14, 15, 17, 13, 12, 18, 11, 5, 16, 17, 6, 13, 5, 12, 4, 8, 18,
        14, 10, 16, 15, 17, 4, 18, 7, 6, 14, 9, 16, 15, 7, 6, 17, 11, 16, 13, 8, 17, 10, 15, 18,
        13, 12, 8, 11, 9, 14, 11, 16, 10, 17, 9, 14, 18, 10, 15, 12, 15, 16, 12, 16, 17, 18, 17, 18,
    ),
)


def streams_of(group, half, n):
    bits = n.bit_length() - 1
    shares = sum(share for share, _ in PLAN[group])
    out, at = [], 0
    for share, order in PLAN[group]:
        rows = half * share // shares
        piece = rows >> scattered(n)
        lands = rows - piece + (bits - scattered(n)) * piece
        out.append((at, rows, lands, [b for b in order if b < bits] + list(range(4, bits))))
        at += rows
    return out


def add_rows(dst, at, src, start, rows):
    block = math.gcd(rows, 128)

    def step(i, carry):
        to = pl.ds(pl.multiple_of(at + i * block, 16), block)
        dst[to, :] = dst[to, :] + src[pl.ds(pl.multiple_of(start + i * block, 16), block), :]
        return carry

    lax.fori_loop(0, rows // block, step, 0)


def sum_steps(here, g, twin_in, ring_in, send, recv, free, half, first, rows, order, owner):
    def remote(i, src, dst, device):
        return pltpu.make_async_remote_copy(
            src_ref=src, dst_ref=dst, send_sem=send, recv_sem=recv.at[i],
            device_id=device, device_id_type=MESH,
        )

    def rows_at(at, count):
        return g.at[pl.ds(pl.multiple_of(at, 16), count)]

    def signal(i, device):
        pl.semaphore_signal(free.at[i], inc=1, device_id=device, device_id_type=MESH)

    mine = here.sec * half + first
    other = (1 - here.sec) * half + first
    index, landing = 0, 0
    copy = remote(index, rows_at(other, rows), twin_in.at[pl.ds(first, rows)], here.twin())
    copy.start()
    yield
    copy.wait()
    signal(0, here.twin())
    add_rows(g, mine, twin_in, first, rows)
    at, length = mine, rows
    trail = []
    for step, b in enumerate(order):
        index += 1
        if step >= 4:
            copy = remote(index, rows_at(at, length), ring_in.at[pl.ds(landing, length)], here.partner(b))
            copy.start()
            yield
            copy.wait()
            add_rows(g, at, ring_in, landing, length)
            landing += length
            continue
        length //= 2
        side = here.side(b)
        keep, give = at + side * length, at + (1 - side) * length
        copy = remote(index, rows_at(give, length), ring_in.at[pl.ds(landing, length)], here.partner(b))
        copy.start()
        yield
        copy.wait()
        signal(1 + step, here.partner(b))
        add_rows(g, keep, ring_in, landing, length)
        trail.append((b, at, length))
        at, landing = keep, landing + length
    for step, (b, before, length) in reversed(list(enumerate(trail))):
        index += 1
        pl.semaphore_wait(free.at[1 + step], 1)
        copy = remote(index, rows_at(at, length), rows_at(at, length), here.partner(b))
        copy.start()
        yield
        copy.wait()
        at = before
    index += 1
    pl.semaphore_wait(free.at[0], 1)
    copy = remote(index, rows_at(mine, rows), rows_at(mine, rows), here.twin())
    if owner is None:
        copy.start()
        yield
        copy.wait()
    else:
        gives = here.sec != owner

        @pl.when(gives)
        def _():
            copy.start()

        yield

        @pl.when(gives)
        def _():
            copy.wait_send()

        @pl.when(jnp.logical_not(gives))
        def _():
            copy.wait_recv()


def fused(n, halves, sents, *refs):
    (
        sl, tl, routes, xroutes, ag, ab, fg, fb, rb, eb, wk, wv, wrt, cg, cb, xwk, xwv, xwrt,
        emb, cot, wq, wo, we, wr, xwq, xwo,
        act_out, gin_out, gff_out, gat_out, gx_out,
        x_v, x_oth, p_v, xp_v, sm_v, xsm_v, wq_v, wo_v, we_v, wr_v, cot_v, xwq_v, xwo_v,
        wsm, kept_refs, low_v, mid_v, mem_v, stage_v, f_v, ft_v, acc, dacc, deb, out_v,
        gff, gx_v, ge_v, gd_v, twin_in, ring_in, sum_send, sum_recv, sum_free,
        own_sem, in_send, in_recv, out_sem, out_send, out_recv,
    ) = refs
    here = Here(n)
    sec = here.sec
    barrier = pltpu.get_barrier_semaphore()
    pl.semaphore_signal(barrier, inc=1, device_id=here.twin(), device_id_type=MESH)
    for b in range(here.bits):
        pl.semaphore_signal(barrier, inc=1, device_id=here.partner(b), device_id_type=MESH)

    def slot(ref, which):
        return ref.at[pl.ds(pl.multiple_of(which * T, T), T)]

    def remote(src, dst, send, recv):
        return pltpu.make_async_remote_copy(
            src_ref=src, dst_ref=dst, send_sem=send, recv_sem=recv, device_id=here.twin(), device_id_type=MESH
        )

    local = {}
    for i, (name, src, dst) in enumerate((
        ("x_oth", slot(emb, 1 - sec), x_oth), ("x", slot(emb, sec), x_v.at[sec]), ("wq", wq, wq_v.at[sec]),
        ("wo", wo, wo_v.at[sec]), ("we", we, we_v.at[sec]), ("wr", wr, wr_v.at[sec]),
        ("xwq", xwq, xwq_v), ("xwo", xwo, xwo_v), ("cot", slot(cot, sec), cot_v),
    )):
        local[name] = pltpu.make_async_copy(src, dst, own_sem.at[i])
        local[name].start()

    def need(*names):
        for name in names:
            local[name].wait()

    own_at = pl.multiple_of(sec * T, T)
    p_v[sec] = small_rows(
        [ref[...] for ref in (ag, ab, fg, fb, rb)]
        + [eb[:, i * D : (i + 1) * D] for i in range(FF // D)]
        + [routes[r : r + 1, m * T : (m + 1) * T].astype(F32) for m in range(2) for r in range(2)]
    )
    xp_v[...] = small_rows(
        [cg[...], cb[...]] + [xroutes[r : r + 1, pl.ds(own_at, T)].astype(F32) for r in range(2)]
    )

    def pack(wk, wv, wrt):
        router = wrt[...].astype(F32)
        tail = jnp.concatenate([router, router, jnp.zeros((16, D), F32)], axis=0).astype(BF16)
        return jnp.concatenate([wk[...], wv[...], tail], axis=0)

    sm_v[sec] = pack(wk, wv, wrt)
    xsm_v[...] = pack(xwk, xwv, xwrt)

    def lay_small(l, ref):
        for i in range(2):
            half = ref[64 * i : 64 * i + 64]
            wsm[l, i] = jnp.concatenate([half, half], axis=0)
        wsm[l, 2] = jnp.concatenate([ref[128:144], jnp.zeros((112, D), BF16)], axis=0)

    def weights(l, small):
        return (
            wq_v.at[l], wsm.at[l, 0], wsm.at[l, 1], small.at[pl.ds(0, PAIR)], wsm.at[l, 2], wo_v.at[l],
        )

    def p(l, i):
        return p_v[l, i : i + 1, :]

    def experts_of(ref, first):
        return [laid_out(ref[first + r : first + r + 1, :]) for r in range(2)]

    kept = [dict(zip([k[0] for k in KEPT], k)) for k in kept_refs]

    lay_small(sec, sm_v.at[sec])

    def own_middle(row, x, dst):
        ends = ends_of([jnp.where(sec == 0, sl[row, i], tl[row, i]) for i in range(sents)])
        allowed = same_of(ends, ends) & (earlier() | (sec == 0))
        x = x[...].astype(F32)
        a = norm(x, p(sec, 0), p(sec, 1)).astype(BF16)
        at = 9 + 2 * row
        experts = [laid_out(p_v[sec, pl.ds(at + r, 1), :]) for r in range(2)]
        dst[...] = x + mixture_fwd(a, a, experts, weights(sec, sm_v.at[sec]), allowed, kept[0])

    swaps = {}
    for i, (name, src, dst) in enumerate((
        ("p", p_v.at[sec], p_v), ("sm", sm_v.at[sec], sm_v), ("we", we, we_v), ("wr", wr, wr_v), ("wq", wq, wq_v),
        ("wo", wo, wo_v), ("x", slot(emb, 1 - sec), x_v),
    )):
        swaps[name] = remote(src, dst.at[sec], in_send.at[i], in_recv.at[i])

    def swapped(*names):
        for name in names:
            swaps[name].wait()

    need("x_oth", "x", "wq", "wo")
    own_middle(1 - sec, x_oth, dacc)
    pl.semaphore_wait(barrier, here.bits + 1)
    for name in ("p", "sm", "we", "wr", "wq", "wo", "x"):
        swaps[name].start()
    own_middle(sec, x_v.at[sec], acc)
    need("we", "wr")
    middle_away = remote(dacc, mid_v.at[1], in_send.at[7], in_recv.at[7])
    memory_away = remote(stage_v, mem_v, in_send.at[8], in_recv.at[8])

    @pl.when(sec == 0)
    def _():
        for f, total in ((f_v, acc), (stage_v, dacc)):
            middle = total[...]
            f[...] = norm(middle, p(0, 2), p(0, 3)).astype(BF16)
            total[...] = middle + p(0, 4)
        feed_fwd(((f_v, acc), (stage_v, dacc)), we_v.at[0], p_v.at[0], wr_v.at[0])
        stage_v[...] = dacc[...].astype(BF16)
        memory_away.start()
        mem_v[...] = acc[...].astype(BF16)

    @pl.when(sec == 1)
    def _():
        middle_away.start()
        mid_v[1] = acc[...]

    need("xwq", "xwo", "cot")
    lay_small(2, xsm_v)

    @pl.when(sec == 0)
    def _():
        middle_away.wait_recv()
        memory_away.wait_send()

    @pl.when(sec == 1)
    def _():
        memory_away.wait_recv()
        middle_away.wait_send()

    finals = []

    def hand_out(start, end):
        start()
        finals.append(end)

    memory_out = [
        pltpu.make_async_copy(ref, act_out.at[pl.ds(m * T, T)], out_sem.at[m]) for m, ref in enumerate((mem_v, stage_v))
    ]

    @pl.when(sec == 0)
    def _():
        for copy in memory_out:
            copy.start()

    s_ends, t_ends = (ends_of([ref[sec, i] for i in range(sents)]) for ref in (sl, tl))
    xw = (xwq_v, wsm.at[2, 0], wsm.at[2, 1], xsm_v.at[pl.ds(0, PAIR)], wsm.at[2, 2], xwo_v)
    c = norm(mid_v[1], xp_v[0:1, :], xp_v[1:2, :]).astype(BF16)
    low_v[1] = c
    mid_v[2] = mid_v[1] + mixture_fwd(c, mem_v[...], experts_of(xp_v, 2), xw, same_of(s_ends, t_ends), kept[1])

    groups = (
        (gff.at[1, 0], 1), (gff.at[1, 1], 1), (gx_v, None), (gff.at[0, 0], 0), (gff.at[0, 1], 0), (ge_v, 0), (gd_v, None),
    )
    live, state = {}, {"stream": 0, "landed": 0, "mark": 0}

    def done(i):
        pairs = {
            0: [(1, gff.at[1, 0], gff_out.at[pl.ds(0, FF)], 3)],
            1: [(1, gff.at[1, 1], gff_out.at[pl.ds(FF, FF)], 4)],
            2: [(None, gx_v, gx_out.at[pl.ds(0, 2 * D)], 5)],
            3: [(0, gff.at[0, 0], gff_out.at[pl.ds(0, FF)], 6)],
            4: [(0, gff.at[0, 1], gff_out.at[pl.ds(FF, FF)], 7)],
            5: [(0, ge_v, gat_out.at[pl.ds(0, 2 * D)], 8)],
            6: [(1, gd_v.at[pl.ds(0, 2 * D)], gat_out.at[pl.ds(0, 2 * D)], 9)]
            + [(l, gd_v.at[pl.ds(2 * D + l * NARROW, NARROW)], gat_out.at[pl.ds(2 * D, NARROW)], 10 + l) for l in range(2)]
            + [(None, gd_v.at[pl.ds(2 * D + 2 * NARROW, NARROW)], gx_out.at[pl.ds(2 * D, NARROW)], 12)],
        }
        for owner, src, dst, sem in pairs[i]:
            copy = pltpu.make_async_copy(src, dst, out_sem.at[sem])
            if owner is None:
                copy.start()
                finals.append(copy.wait)
            else:
                pl.when(sec == owner)(copy.start)
                finals.append(functools.partial(pl.when(sec == owner), copy.wait))

    def advance(k):
        if k in live and next(live[k][1], 1):
            i = live.pop(k)[0]
            if all(entry[0] != i for entry in live.values()):
                done(i)

    def begin(i):
        for k in [k for k in live if live[k][0] == i - 1 and live[k][2] == 0]:
            advance(k)
            live[k][2] = 1
        g, owner = groups[i]
        half = halves[i]
        for first, rows, lands, order in streams_of(i, half, n):
            k = state["stream"]
            stream = sum_steps(
                here, g, twin_in.at[i % 2], ring_in.at[pl.ds(state["landed"], lands)],
                sum_send.at[k], sum_recv.at[k], sum_free.at[k], half, first, rows, order, owner,
            )
            next(stream)
            live[k] = [i, stream, 0]
            state["stream"] += 1
            state["landed"] += lands

    def mark():
        for k in MARKS[state["mark"]]:
            if k in live:
                live[k][2] = 1
                advance(k)
        state["mark"] += 1

    def feed_start(l, middle):
        f = norm(middle, p(l, 2), p(l, 3))
        f_v[...] = f.astype(BF16)
        ft_v[...] = f.T.astype(BF16)
        dacc[...] = jnp.zeros_like(dacc)

    def feed_part(l, part, total):
        feed_both(part, f_v, ft_v, cot_v, we_v.at[l], p_v.at[l], wr_v.at[l], total, dacc, gff.at[l, part], deb.at[l])

    def feed_end(l, middle):
        dend = cot_v[...].astype(F32)
        dmid, dgain, dbias = norm_back(dacc[...], middle, p(l, 2))
        return dmid + dend, [dgain, dbias, jnp.sum(dend, axis=0, keepdims=True)]

    swapped("p", "sm", "we", "wr")
    acc[...] = mid_v[2] + p(1, 4)
    feed_start(1, mid_v[2])
    feed_part(1, 0, acc)
    begin(0)
    feed_part(1, 1, acc)
    begin(1)
    out_v[...] = acc[...].astype(BF16)
    acc[...], feed_small = feed_end(1, mid_v[2])
    mark()
    own_rows = act_out.at[pl.ds(own_at, T)]
    out_near = pltpu.make_async_copy(out_v, own_rows, out_sem.at[2])
    out_away = remote(out_v, own_rows, out_send.at[0], out_recv.at[0])
    pl.when(sec == 1)(out_near.start)
    pl.when(sec == 0)(out_away.start)

    def narrow_tail(l, rows):
        at = 2 * D + l * NARROW + NARROW - 16
        gd_v[at : at + 16, :] = small_rows(rows).astype(BF16)

    dc, dmem = mixture_bwd(
        acc[...].astype(BF16), low_v[1], mem_v[...], experts_of(xp_v, 2), xw, same_of(s_ends, t_ends), kept[1],
        gx_v, 0, gd_v, 2 * D + 2 * NARROW, mark,
    )
    cot_v[...] = dmem.astype(BF16)
    dbefore, dgain, dbias = norm_back(dc, mid_v[1], xp_v[0:1, :])
    narrow_tail(2, [dgain, dbias])
    mid_v[2] = acc[...] + dbefore
    begin(2)
    mark()

    def self_fwd(l, with_out):
        x = x_v[l].astype(F32)
        a = norm(x, p(l, 0), p(l, 1)).astype(BF16)
        low_v[0] = a
        at = 9 + 2 * sec
        experts = [laid_out(p_v[l, pl.ds(at + r, 1), :]) for r in range(2)]
        ends = t_ends if l else s_ends
        allowed = same_of(ends, ends)
        allowed = allowed & earlier() if l else allowed
        out = mixture_fwd(a, a, experts, weights(l, sm_v.at[l]), allowed, kept[0], with_out)
        return x + out if with_out else None

    def self_back(l, grad, wide, feed_small):
        at = 9 + 2 * sec
        experts = [laid_out(p_v[l, pl.ds(at + r, 1), :]) for r in range(2)]
        ends = t_ends if l else s_ends
        allowed = same_of(ends, ends)
        allowed = allowed & earlier() if l else allowed
        da, ds = mixture_bwd(
            grad[...].astype(BF16), low_v[0], low_v[0], experts, weights(l, sm_v.at[l]), allowed, kept[0],
            wide, 0, gd_v, 2 * D + l * NARROW, mark,
        )
        dx, dgain, dbias = norm_back(da + ds, x_v[l].astype(F32), p(l, 0))
        mid_v[l] = grad[...] + dx
        narrow_tail(l, [dgain, dbias] + feed_small + [deb[l, i : i + 1, :] for i in range(FF // D)])

    swapped("wq", "wo", "x")
    lay_small(1 - sec, sm_v.at[1 - sec])
    mid_v[0] = self_fwd(0, True)
    mark()
    feed_start(0, mid_v[0])
    feed_part(0, 0, None)
    begin(3)
    mark()
    feed_part(0, 1, None)
    begin(4)
    acc[...], own_small = feed_end(0, mid_v[0])
    mark()
    self_back(0, acc, ge_v, own_small)
    begin(5)
    mark()

    self_fwd(1, False)
    mark()
    self_back(1, mid_v.at[2], gd_v, feed_small)
    at = 2 * D + 3 * NARROW
    gd_v[at:, :] = jnp.zeros((2 * halves[6] - at, D), BF16)
    begin(6)
    gin_rows = gin_out.at[pl.ds(own_at, T)]
    gin_near = pltpu.make_async_copy(mid_v.at[sec], gin_rows, out_sem.at[13])
    gin_away = remote(mid_v.at[1 - sec], gin_rows, out_send.at[1], out_recv.at[1])
    gin_near.start()
    gin_away.start()
    mark()
    mark()
    while live:
        for k in list(live):
            advance(k)
    for wait in finals:
        wait()
    gin_near.wait()
    gin_away.wait()

    @pl.when(sec == 0)
    def _():
        out_away.wait_send()
        for copy in memory_out:
            copy.wait()

    @pl.when(sec == 1)
    def _():
        out_away.wait_recv()
        out_near.wait()


def widen(act, gin, gff, gat, gx, *refs):
    outs, (act_v, gin_v, gff_v, gat_v, gx_v, ex_v, re_v, mats, in_sem, out_sem) = refs[:-10], refs[-10:]
    act_out, gin_out, expand, reduce, q, o, xq, xo = outs[:8]
    smalls = outs[8:]
    loads, at = [], 0
    for ref, dst in ((gff, gff_v), (gat, gat_v), (gx, gx_v)):
        for first in range(0, ref.shape[0], D):
            rows = pl.ds(first, min(D, ref.shape[0] - first))
            loads.append(pltpu.make_async_copy(ref.at[rows], dst.at[rows], in_sem.at[at]))
            loads[-1].start()
            at += 1
    passing = [
        pltpu.make_async_copy(a, b, in_sem.at[at + i]) for i, (a, b) in enumerate(((act, act_v), (gin, gin_v)))
    ]
    for copy in passing:
        copy.start()
    stores = []

    def store(src, dst):
        stores.append(pltpu.make_async_copy(src, dst, out_sem.at[len(stores)]))
        stores[-1].start()

    blocks = PART // D
    for i in range(2 * FF // D):
        loads[i].wait()
        part, kind, block = i // (2 * blocks), (i // blocks) % 2, i % blocks
        col = part * PART + block * D
        value = gff_v[i * D : (i + 1) * D, :].astype(F32)
        if kind == 0:
            ex_v[:, col : col + D] = value
            store(ex_v.at[:, pl.ds(col, D)], expand.at[:, pl.ds(col, D)])
        else:
            re_v[col : col + D, :] = value
            store(re_v.at[pl.ds(col, D)], reduce.at[pl.ds(col, D)])
    i = 2 * FF // D
    for m, (src, row, dst) in enumerate(((gat_v, 0, q), (gat_v, D, o), (gx_v, 0, xq), (gx_v, D, xo))):
        loads[i + m + m // 2].wait()
        mats[m] = src[row : row + D, :].astype(F32)
        store(mats.at[m], dst)
    for k, load in enumerate((loads[i + 2], loads[i + 5])):
        load.wait()
        src = (gat_v, gx_v)[k]
        ks, vs, rs = smalls[:3] if k == 0 else smalls[9:12]
        at = 2 * D
        ks[...] = src[at : at + 64, :].astype(F32)
        vs[...] = src[at + 64 : at + PAIR, :].astype(F32)
        rs[...] = src[at + PAIR : at + PAIR + 16, :].astype(F32)[0:8]
        tail = src[at + PAIR + 16 : at + NARROW, :].astype(F32)
        if k == 0:
            for j in range(5):
                smalls[3 + j][...] = tail[j : j + 1]
            for j in range(FF // D):
                smalls[8][:, j * D : (j + 1) * D] = tail[5 + j : 6 + j]
        else:
            for j in range(2):
                smalls[12 + j][...] = tail[j : j + 1]
    for copy, src, dst in zip(passing, (act_v, gin_v), (act_out, gin_out)):
        copy.wait()
        store(src, dst)
    for copy in stores:
        copy.wait()


def body(n, *arrays):
    (
        embeddings, cotangent, source_lengths, target_lengths, self_routes, cross_routes,
        attend_gain, attend_bias, self_router, query_weight, key_weight, value_weight, output_weight,
        feed_gain, feed_bias, expand_weight, expand_bias, reduce_weight, reduce_bias,
        cross_gain, cross_bias, cross_router, cross_query, cross_key, cross_value, cross_output,
    ) = arrays
    row_count = embeddings.shape[1]
    sents = source_lengths.shape[1]
    part = up(PART, n)
    halves = (part, part, up(D, n), part, part, up(D, n), up((2 * D + 3 * NARROW + 1) // 2, n))
    cut = [stream for i, half in enumerate(halves) for stream in streams_of(i, half, n)]
    streams, lands = len(cut), sum(stream[2] for stream in cut)
    steps = n.bit_length() - 1 + scattered(n) + 2
    S, V, DMA = jax.ShapeDtypeStruct, pltpu.VMEM, pltpu.SemaphoreType.DMA
    hbm, smem = pl.BlockSpec(memory_space=pl.ANY), pl.BlockSpec(memory_space=pltpu.SMEM)
    vmem = pl.BlockSpec(memory_space=pltpu.VMEM)
    rows = 2 * D + NARROW
    act, gin, gff, gat, gx = pl.pallas_call(
        functools.partial(fused, n, halves, sents),
        in_specs=[smem] * 2 + [vmem] * 16 + [hbm] * 8,
        out_specs=[hbm] * 5,
        out_shape=[
            S((row_count, D), BF16), S((row_count, D), F32),
            S((2 * FF, D), BF16), S((rows, D), BF16), S((rows, D), BF16),
        ],
        scratch_shapes=[
            V((2, T, D), BF16), V((T, D), BF16), V((2, 16, D), F32), V((16, D), F32), V((2, NARROW, D), BF16), V((NARROW, D), BF16),
            V((2, D, D), BF16), V((2, D, D), BF16), V((2, D, FF), BF16), V((2, FF, D), BF16),
            V((T, D), BF16), V((D, D), BF16), V((D, D), BF16),
            V((3, 3, PAIR, D), BF16), [[V(s, t) for _, s, t in KEPT] for _ in range(2)],
            V((2, T, D), BF16), V((3, T, D), F32), V((T, D), BF16), V((T, D), BF16), V((T, D), BF16), V((D, T), BF16),
            V((T, D), F32), V((T, D), F32), V((2, 8, D), F32), V((T, D), BF16),
            V((2, PARTS, 2 * part, D), BF16), *(V((2 * halves[i], D), BF16) for i in (2, 5, 6)),
            V((2, max(halves), D), BF16), V((lands, D), BF16), DMA((streams,)), DMA((streams, steps)),
            pltpu.SemaphoreType.REGULAR((streams, 1 + scattered(n))),
            DMA((9,)), DMA((9,)), DMA((9,)), DMA((14,)), DMA((2,)), DMA((2,)),
        ],
        compiler_params=pltpu.CompilerParams(
            collective_id=0, has_side_effects=True, vmem_limit_bytes=(63 << 20) + (900 << 10)
        ),
    )(
        source_lengths, target_lengths, self_routes[0].T, cross_routes.T,
        attend_gain, attend_bias, feed_gain, feed_bias, reduce_bias, expand_bias,
        key_weight[0].T, value_weight[0].T, self_router[0].T,
        cross_gain[None], cross_bias[None], cross_key.T, cross_value.T, cross_router.T,
        embeddings[0], cotangent, query_weight[0], output_weight[0], expand_weight[0], reduce_weight[0],
        cross_query, cross_output,
    )
    wide = [(row_count, D), (row_count, D), (D, FF), (FF, D)] + [(D, D)] * 4
    narrow = [(64, D), (64, D), (8, D)] + [(1, D)] * 5 + [(1, FF)] + [(64, D), (64, D), (8, D)] + [(1, D)] * 2
    out = pl.pallas_call(
        widen,
        in_specs=[hbm] * 5,
        out_specs=[hbm] * len(wide) + [vmem] * len(narrow),
        out_shape=[S(s, BF16 if i == 0 else F32) for i, s in enumerate(wide + narrow)],
        scratch_shapes=[
            V((row_count, D), BF16), V((row_count, D), F32), V((2 * FF, D), BF16), V((rows, D), BF16), V((rows, D), BF16),
            V((D, FF), F32), V((FF, D), F32), V((4, D, D), F32), DMA((2 * FF // D + 8,)), DMA((2 * FF // D + 6,)),
        ],
        compiler_params=pltpu.CompilerParams(vmem_limit_bytes=(63 << 20) + (900 << 10)),
    )(act, gin, gff, gat, gx)
    act, gin, expand, reduce, q, o, xq, xo = out[:8]
    k, v, r, gains, biases, fgain, fbias, rbias, ebias, xk, xv, xr, xgain, xbias = out[8:]
    return (
        act[None], gin[None], gains, biases, r.T[None], q[None], k.T[None], v.T[None], o[None],
        fgain, fbias, expand[None], ebias, reduce[None], rbias,
        xgain[0], xbias[0], xr.T, xq, xk.T, xv.T, xo,
    )


def solution(mesh):
    n = mesh.shape["dp"]
    stacked, rows = P("section", None), P("dp", None)
    matrix, both = P("section", None, None), P("section", "dp", None)
    params = (
        stacked, stacked, matrix, matrix, matrix, matrix, matrix, stacked, stacked, matrix, stacked, matrix, stacked,
    ) + (P(),) * 7
    return jax.shard_map(
        functools.partial(body, n),
        mesh=mesh,
        in_specs=(both, rows, rows, rows, both, rows) + params,
        out_specs=(both, both) + params,
        check_vma=False,
    )
```

```python
import functools
import math

import jax
import jax.numpy as jnp
from jax import lax
from jax.experimental import pallas as pl
from jax.experimental.pallas import tpu as pltpu
from jax.sharding import PartitionSpec as P

EPSILON = 1e-05
SCORE_SCALE = 0.125
MASKED_SCORE = -1000000000.0
F32 = jnp.float32
BF16 = jnp.bfloat16
T = 512
D = 512
FF = 2048
PAIR = 128
CH = 512
PARTS = 2
PART = FF // PARTS
NARROW = 160
MESH = pl.DeviceIdType.MESH


def dot(a, b):
    return lax.dot_general(a, b, (((1,), (0,)), ((), ())), preferred_element_type=F32)


def dot_nt(a, b):
    return lax.dot_general(a, b, (((1,), (1,)), ((), ())), preferred_element_type=F32)


def dot_tn(a, b):
    return lax.dot_general(a, b, (((0,), (0,)), ((), ())), preferred_element_type=F32)


def iota(shape, axis):
    return lax.broadcasted_iota(jnp.int32, shape, axis)


def norm_parts(v):
    centred = v - jnp.mean(v, axis=-1, keepdims=True)
    spread = jnp.mean(centred * centred, axis=-1, keepdims=True)
    return centred, lax.rsqrt(spread + EPSILON)


def norm(v, gain, bias):
    centred, scale = norm_parts(v)
    return centred * scale * gain + bias


def norm_back(dn, v, gain):
    centred, scale = norm_parts(v)
    unit = centred * scale
    dgain = jnp.sum(dn * unit, axis=0, keepdims=True)
    dbias = jnp.sum(dn, axis=0, keepdims=True)
    dunit = dn * gain
    first = jnp.mean(dunit, axis=-1, keepdims=True)
    second = jnp.mean(dunit * unit, axis=-1, keepdims=True)
    return scale * (dunit - first - unit * second), dgain, dbias


def ids_of(ends, shape, axis):
    places = iota(shape, axis)
    total = jnp.zeros(shape, jnp.int32)
    for end in ends:
        total = total + (places >= end).astype(jnp.int32)
    return total


def ends_of(lengths):
    ends, total = [], jnp.int32(0)
    for length in lengths:
        total = total + length
        ends.append(total)
    return ends


def same_of(key_ends, query_ends):
    return ids_of(key_ends, (T, 1), 0) == ids_of(query_ends, (1, T), 1)


def earlier():
    return iota((T, T), 0) <= iota((T, T), 1)


def chosen(expert, block):
    return expert == (iota((T, PAIR), 1) // 64 + 2 * block).astype(F32)


def laid_out(row):
    return jnp.broadcast_to(row, (PAIR, T)).T


def mixture_fwd(a, s, experts, w, allowed, kept, with_out=True):
    wq, wk2, wv2, wkv, wr2, wo = w
    q = dot(a, wq[...])
    logits = dot_nt(a, wr2[...])
    kk = dot_nt(s, wk2[...]).astype(BF16)
    vv = dot_nt(s, wv2[...]).astype(BF16)
    kept["kk"][...] = kk
    kept["vv"][...] = vv
    lanes = iota((T, PAIR), 1).astype(F32)
    raised = [
        jnp.exp(jnp.sum(jnp.where(lanes == e, logits, 0.0), axis=-1, keepdims=True))
        for e in experts
    ]
    total = raised[0] + raised[1]
    gated = [jnp.zeros((T, PAIR), F32) for _ in range(4)]
    for r in range(2):
        gate = raised[r] / total
        kept["gate"][r] = jnp.broadcast_to(gate, (T, PAIR))
        qs = jnp.zeros((T, PAIR), F32)
        for b in range(4):
            qs = jnp.where(chosen(experts[r], b), q[:, b * PAIR : (b + 1) * PAIR], qs)
        qs = qs.astype(BF16)
        kept["qs"][r] = qs
        scores = jnp.where(allowed, dot_nt(kk, qs) * SCORE_SCALE, MASKED_SCORE)
        top = jnp.max(scores, axis=0, keepdims=True)
        p = jnp.exp(scores - top)
        inverse = 1.0 / jnp.sum(p, axis=0, keepdims=True)
        kept["top"][r : r + 1] = top
        kept["inv"][r : r + 1] = inverse
        chance = (p * inverse).astype(BF16)
        mixed = dot_tn(vv, chance).T
        kept["mixed"][r] = mixed
        weighted = gate * mixed
        for b in range(4):
            gated[b] = jnp.where(chosen(experts[r], b), weighted, gated[b])
    for b in range(4):
        kept["gated"][:, b * PAIR : (b + 1) * PAIR] = gated[b].astype(BF16)
    if with_out:
        return dot(kept["gated"][...], wo[...])


def mixture_bwd(dy, a, s, experts, w, allowed, kept, wide, base, narrow, nbase, mark):
    wq, wk2, wv2, wkv, wr2, wo = w
    wide[base + D : base + 2 * D, :] = dot_tn(kept["gated"][...], dy).astype(BF16)
    dgated = dot_nt(dy, wo[...]).astype(BF16).astype(F32)
    kk, vv = kept["kk"][...], kept["vv"][...]
    lanes = iota((T, PAIR), 1)
    dkk = jnp.zeros((T, PAIR), F32)
    dvv = jnp.zeros((T, PAIR), F32)
    dgates, gates, dqs = [], [], []
    for r in range(2):
        own = jnp.zeros((T, PAIR), F32)
        for b in range(4):
            own = jnp.where(chosen(experts[r], b), dgated[:, b * PAIR : (b + 1) * PAIR], own)
        gate = kept["gate"][r]
        gates.append(gate)
        dgates.append(jnp.sum(own * kept["mixed"][r], axis=-1, keepdims=True))
        dmixed = (gate * own).astype(BF16)
        qs = kept["qs"][r]
        scores = jnp.where(allowed, dot_nt(kk, qs) * SCORE_SCALE, MASKED_SCORE)
        p = jnp.exp(scores - kept["top"][r : r + 1]) * kept["inv"][r : r + 1]
        dp = dot_nt(vv, dmixed)
        both = jnp.sum(p * dp, axis=0, keepdims=True)
        ds = (p * (dp - both)).astype(BF16)
        dkk = dkk + dot(ds, qs)
        dvv = dvv + dot(p.astype(BF16), dmixed)
        dqs.append((dot_tn(kk, ds) * SCORE_SCALE).T)
        mark()
    dq = []
    for b in range(4):
        part = jnp.zeros((T, PAIR), F32)
        for r in range(2):
            part = jnp.where(chosen(experts[r], b), dqs[r], part)
        dq.append(part.astype(BF16))
    dq = jnp.concatenate(dq, axis=1)
    dk = (dkk + pltpu.roll(dkk, 64, 1)) * SCORE_SCALE
    dv = dvv + pltpu.roll(dvv, 64, 1)
    dkv = jnp.where(lanes < 64, dk, dv).astype(BF16)
    mean = gates[0] * dgates[0] + gates[1] * dgates[1]
    dl = jnp.zeros((T, PAIR), F32)
    for r in range(2):
        dl = jnp.where(((lanes % 8).astype(F32) == experts[r]) & (lanes < 16), gates[r] * (dgates[r] - mean), dl)
    high = dl.astype(BF16).astype(F32)
    dl = jnp.where(lanes < 8, high, dl - high).astype(BF16)
    wide[base : base + D, :] = dot_tn(a, dq).astype(BF16)
    narrow[nbase : nbase + PAIR, :] = dot_tn(dkv, s).astype(BF16)
    dwr = dot_tn(dl, a)
    dwr = dwr[0:8] + dwr[8:16]
    narrow[nbase + PAIR : nbase + PAIR + 16, :] = jnp.concatenate([dwr, jnp.zeros((8, D), F32)], axis=0).astype(BF16)
    da = dot_nt(dq, wq[...]) + dot(dl, wr2[...])
    ds = dot(dkv, wkv[...])
    return da, ds


C0, C1 = 0.7978845608028654, 0.044715


def gelu(pre):
    half = 0.5 * jnp.tanh(C0 * (pre + C1 * pre * pre * pre)) + 0.5
    return pre * half


def gelu_both(pre):
    square = pre * pre
    t = jnp.tanh(C0 * pre * (1.0 + C1 * square))
    half = 0.5 * t + 0.5
    slope = half + 0.5 * pre * (1.0 - t * t) * (C0 * (1.0 + 3.0 * C1 * square))
    return pre * half, slope


def expand_step(j, f, we, p):
    at = pl.multiple_of(j * CH, CH)
    return dot(f[...], we[:, pl.ds(at, CH)]) + p[pl.ds(5 + j, 1), :]


def feed_fwd(pairs, we, p, wr):
    def step(j, carry):
        at = pl.multiple_of(j * CH, CH)
        for f, acc in pairs:
            hidden = gelu(expand_step(j, f, we, p)).astype(BF16)
            acc[...] += dot(hidden, wr[pl.ds(at, CH), :])
        return carry

    lax.fori_loop(0, FF // CH, step, 0)


def small_rows(rows, count=16):
    places = iota((count, D), 0)
    out = jnp.zeros((count, D), F32)
    for i, row in enumerate(rows):
        out = jnp.where(places == i, row, out)
    return out


KEPT = (
    ("kk", (T, PAIR), BF16),
    ("vv", (T, PAIR), BF16),
    ("gate", (2, T, PAIR), F32),
    ("qs", (2, T, PAIR), BF16),
    ("top", (8, T), F32),
    ("inv", (8, T), F32),
    ("mixed", (2, T, PAIR), F32),
    ("gated", (T, D), BF16),
)


class Here:
    def __init__(self, n):
        self.bits = n.bit_length() - 1
        self.sec = lax.axis_index("section")
        self.rank = lax.axis_index("dp")

    def side(self, b):
        return lax.rem(self.rank // (1 << b), 2)

    def partner(self, b):
        return (self.sec, self.rank + (1 - 2 * self.side(b)) * (1 << b))

    def twin(self):
        return (1 - self.sec, self.rank)


def scattered(n):
    return min(4, n.bit_length() - 1)


def up(rows, n):
    unit = 16 << scattered(n)
    return -(-rows // unit) * unit


PLAN = (
    ((1, (1, 0, 2, 3)), (2, (2, 0, 1, 3)), (1, (0, 3, 1, 2))),
    ((1, (0, 1, 2, 3)), (2, (0, 1, 2, 3)), (1, (1, 3, 2, 0))),
    ((1, (1, 0, 2, 3)), (1, (3, 0, 1, 2))),
    ((2, (0, 1, 2, 3)), (1, (1, 3, 0, 2)), (1, (0, 1, 2, 3))),
    ((1, (1, 0, 2, 3)), (2, (2, 0, 1, 3)), (1, (0, 1, 2, 3))),
    ((1, (1, 0, 2, 3)), (1, (2, 1, 0, 3))),
    ((1, (1, 0, 3, 2)), (1, (0, 1, 2, 3)), (1, (0, 1, 2, 3))),
)
MARKS = (
    (),
    (),
    (),
    (0,),
    (2,),
    (1, 3, 5, 2, 4, 0, 6),
    (7, 11, 12, 13),
    (9,),
    (3, 0, 2, 8, 5),
    (4, 10),
    (14, 15, 11, 1),
    (12, 6, 3),
    (7, 8, 2, 9, 10, 0, 5, 13, 4, 11, 14),
    (
        15, 1, 6, 16, 12, 17, 3, 18, 7, 9, 8, 5, 2, 10, 13, 0, 14, 11, 15, 4, 7, 1, 9, 6,
        17, 16, 3, 13, 12, 8, 2, 0, 10, 18, 14, 5, 17, 7, 11, 15, 9, 4, 16, 3, 18, 1, 0, 7,
        5, 6, 9, 13, 17, 3, 12, 1, 8, 7, 4, 18, 0, 2, 6, 10, 3, 14, 11, 0, 4, 15, 8, 1,
        3, 16, 10, 11, 2, 5, 6, 8, 2, 9, 10, 13, 17, 12, 5, 4, 11, 5, 6, 4, 1, 6, 7, 16,
        9, 18, 13, 14, 12, 1, 15, 8, 7, 17, 9, 16, 18, 11, 14, 10, 8, 13, 17, 11, 16, 18, 10, 12,
        15, 17, 14, 18, 15, 13, 16, 13, 14, 12, 17, 14, 12, 15, 16, 17, 18, 15, 16, 18,
    ),
)


def streams_of(group, half, n):
    bits = n.bit_length() - 1
    shares = sum(share for share, _ in PLAN[group])
    out, at = [], 0
    for share, order in PLAN[group]:
        rows = half * share // shares
        piece = rows >> scattered(n)
        lands = rows - piece + (bits - scattered(n)) * piece
        out.append((at, rows, lands, [b for b in order if b < bits] + list(range(4, bits))))
        at += rows
    return out


def add_rows(dst, at, src, start, rows):
    block = math.gcd(rows, 128)

    def step(i, carry):
        to = pl.ds(pl.multiple_of(at + i * block, 16), block)
        dst[to, :] = dst[to, :] + src[pl.ds(pl.multiple_of(start + i * block, 16), block), :]
        return carry

    lax.fori_loop(0, rows // block, step, 0)


def sum_steps(here, g, twin_in, ring_in, send, recv, free, half, first, rows, order, owner):
    def remote(i, src, dst, device):
        return pltpu.make_async_remote_copy(
            src_ref=src, dst_ref=dst, send_sem=send, recv_sem=recv.at[i],
            device_id=device, device_id_type=MESH,
        )

    def rows_at(at, count):
        return g.at[pl.ds(pl.multiple_of(at, 16), count)]

    def signal(i, device):
        pl.semaphore_signal(free.at[i], inc=1, device_id=device, device_id_type=MESH)

    def summed(copy, credit, device, at, source, start, length):
        def end():
            copy.wait()
            if credit is not None:
                signal(credit, device)
            add_rows(g, at, source, start, length)

        return end

    def after(credit, copy):
        def start():
            pl.semaphore_wait(free.at[credit], 1)
            copy.start()

        return start

    mine = here.sec * half + first
    other = (1 - here.sec) * half + first
    copies = 0
    copy = remote(copies, rows_at(other, rows), twin_in.at[pl.ds(first, rows)], here.twin())
    moves = [(copy.start, summed(copy, 0, here.twin(), mine, twin_in, first, rows))]
    at, length, landing, trail = mine, rows, 0, []
    for step, b in enumerate(order):
        copies += 1
        partner = here.partner(b)
        if step >= 4:
            copy = remote(copies, rows_at(at, length), ring_in.at[pl.ds(landing, length)], partner)
            moves.append((copy.start, summed(copy, None, partner, at, ring_in, landing, length)))
            landing += length
            continue
        length //= 2
        side = here.side(b)
        keep, give = at + side * length, at + (1 - side) * length
        copy = remote(copies, rows_at(give, length), ring_in.at[pl.ds(landing, length)], partner)
        moves.append((copy.start, summed(copy, 1 + step, partner, keep, ring_in, landing, length)))
        trail.append((b, at, length))
        at, landing = keep, landing + length
    for step, (b, before, length) in reversed(list(enumerate(trail))):
        copies += 1
        copy = remote(copies, rows_at(at, length), rows_at(at, length), here.partner(b))
        moves.append((after(1 + step, copy), copy.wait))
        at = before
    copies += 1
    copy = remote(copies, rows_at(mine, rows), rows_at(mine, rows), here.twin())
    if owner is None:
        moves.append((after(0, copy), copy.wait))
    else:
        gives = here.sec != owner

        def start():
            pl.semaphore_wait(free.at[0], 1)
            pl.when(gives)(copy.start)

        def end():
            pl.when(gives)(copy.wait_send)
            pl.when(jnp.logical_not(gives))(copy.wait_recv)

        moves.append((start, end))
    ends = [end for _, end in moves]
    starts = [start for start, _ in moves[1:]]

    def both(end, start):
        def step():
            end()
            start()

        return step

    return [moves[0][0]] + [both(end, start) for end, start in zip(ends, starts)] + [ends[-1]]


def fused(n, halves, sents, *refs):
    (
        sl, tl, routes, xroutes, ag, ab, fg, fb, rb, eb, wk, wv, wrt, cg, cb, xwk, xwv, xwrt,
        emb, cot, wq, wo, we, wr, xwq, xwo,
        act_out, gin_out, gff_out, gat_out, gx_out,
        x_v, p_v, xp_v, sm_v, xsm_v, wq_v, wo_v, we_v, wr_v, cot_v, xwq_v, xwo_v,
        wsm, kept_refs, low_v, mid_v, mem_v, stage_v, f_v, ft_v, totals, deb, out_v,
        gff, gx_v, ge_v, gd_v, twin_in, ring_in, sum_send, sum_recv, sum_free,
        own_sem, in_send, in_recv, out_sem, out_send, out_recv,
    ) = refs
    here = Here(n)
    sec = here.sec
    acc, dacc = totals.at[0], totals.at[1]
    barrier = pltpu.get_barrier_semaphore()
    pl.semaphore_signal(barrier, inc=1, device_id=here.twin(), device_id_type=MESH)
    for b in range(here.bits):
        pl.semaphore_signal(barrier, inc=1, device_id=here.partner(b), device_id_type=MESH)

    def slot(ref, which):
        return ref.at[pl.ds(pl.multiple_of(which * T, T), T)]

    def remote(src, dst, send, recv):
        return pltpu.make_async_remote_copy(
            src_ref=src, dst_ref=dst, send_sem=send, recv_sem=recv, device_id=here.twin(), device_id_type=MESH
        )

    local = {}
    for i, (name, src, dst) in enumerate((
        ("x_oth", slot(emb, 1 - sec), x_v.at[2]), ("x", slot(emb, sec), x_v.at[sec]), ("wq", wq, wq_v.at[sec]),
        ("wo", wo, wo_v.at[sec]), ("we", we, we_v.at[sec]), ("wr", wr, wr_v.at[sec]),
        ("xwq", xwq, xwq_v), ("xwo", xwo, xwo_v), ("cot", slot(cot, sec), cot_v),
    )):
        local[name] = pltpu.make_async_copy(src, dst, own_sem.at[i])
        local[name].start()

    def need(*names):
        for name in names:
            local[name].wait()

    own_at = pl.multiple_of(sec * T, T)
    p_v[sec] = small_rows(
        [ref[...] for ref in (ag, ab, fg, fb, rb)]
        + [eb[:, i * D : (i + 1) * D] for i in range(FF // D)]
        + [routes[r : r + 1, m * T : (m + 1) * T].astype(F32) for m in range(2) for r in range(2)]
    )
    xp_v[...] = small_rows(
        [cg[...], cb[...]] + [xroutes[r : r + 1, pl.ds(own_at, T)].astype(F32) for r in range(2)]
    )

    def pack(wk, wv, wrt):
        router = wrt[...].astype(F32)
        tail = jnp.concatenate([router, router, jnp.zeros((16, D), F32)], axis=0).astype(BF16)
        return jnp.concatenate([wk[...], wv[...], tail], axis=0)

    sm_v[sec] = pack(wk, wv, wrt)
    xsm_v[...] = pack(xwk, xwv, xwrt)

    def lay_small(l, ref):
        for i in range(2):
            half = ref[64 * i : 64 * i + 64]
            wsm[l, i] = jnp.concatenate([half, half], axis=0)
        wsm[l, 2] = jnp.concatenate([ref[128:144], jnp.zeros((112, D), BF16)], axis=0)

    def weights(l, small):
        return (
            wq_v.at[l], wsm.at[l, 0], wsm.at[l, 1], small.at[pl.ds(0, PAIR)], wsm.at[l, 2], wo_v.at[l],
        )

    def p(l, i):
        return p_v[l, i : i + 1, :]

    def experts_of(ref, first):
        return [laid_out(ref[first + r : first + r + 1, :]) for r in range(2)]

    kept = [dict(zip([k[0] for k in KEPT], k)) for k in kept_refs]

    lay_small(sec, sm_v.at[sec])

    def own_middle(i, carry):
        row = jnp.where(i == 0, 1 - sec, sec)
        ends = ends_of([jnp.where(sec == 0, sl[row, i], tl[row, i]) for i in range(sents)])
        allowed = same_of(ends, ends) & (earlier() | (sec == 0))
        x = x_v[jnp.where(i == 0, 2, sec)].astype(F32)
        a = norm(x, p(sec, 0), p(sec, 1)).astype(BF16)
        at = 9 + 2 * row
        experts = [laid_out(p_v[sec, pl.ds(at + r, 1), :]) for r in range(2)]
        totals[1 - i] = x + mixture_fwd(a, a, experts, weights(sec, sm_v.at[sec]), allowed, kept[0])

        @pl.when(i == 0)
        def _():
            pl.semaphore_wait(barrier, here.bits + 1)
            for name in ("p", "sm", "we", "wr", "wq", "wo", "x"):
                swaps[name].start()

        return carry

    swaps = {}
    for i, (name, src, dst) in enumerate((
        ("p", p_v.at[sec], p_v), ("sm", sm_v.at[sec], sm_v), ("we", we, we_v), ("wr", wr, wr_v), ("wq", wq, wq_v),
        ("wo", wo, wo_v), ("x", slot(emb, 1 - sec), x_v),
    )):
        swaps[name] = remote(src, dst.at[sec], in_send.at[i], in_recv.at[i])

    def swapped(*names):
        for name in names:
            swaps[name].wait()

    need("x_oth", "x", "wq", "wo")
    lax.fori_loop(0, 2, own_middle, 0)
    need("we", "wr")
    middle_away = remote(dacc, mid_v.at[1], in_send.at[7], in_recv.at[7])
    memory_away = remote(stage_v, mem_v, in_send.at[8], in_recv.at[8])

    @pl.when(sec == 0)
    def _():
        for f, total in ((f_v, acc), (stage_v, dacc)):
            middle = total[...]
            f[...] = norm(middle, p(0, 2), p(0, 3)).astype(BF16)
            total[...] = middle + p(0, 4)
        feed_fwd(((f_v, acc), (stage_v, dacc)), we_v.at[0], p_v.at[0], wr_v.at[0])
        stage_v[...] = dacc[...].astype(BF16)
        memory_away.start()
        mem_v[...] = acc[...].astype(BF16)

    @pl.when(sec == 1)
    def _():
        middle_away.start()
        mid_v[1] = acc[...]

    need("xwq", "xwo", "cot")
    lay_small(2, xsm_v)

    @pl.when(sec == 0)
    def _():
        middle_away.wait_recv()
        memory_away.wait_send()

    @pl.when(sec == 1)
    def _():
        memory_away.wait_recv()
        middle_away.wait_send()

    finals = []

    def hand_out(start, end):
        start()
        finals.append(end)

    memory_out = [
        pltpu.make_async_copy(ref, act_out.at[pl.ds(m * T, T)], out_sem.at[m]) for m, ref in enumerate((mem_v, stage_v))
    ]

    @pl.when(sec == 0)
    def _():
        for copy in memory_out:
            copy.start()

    s_ends, t_ends = (ends_of([ref[sec, i] for i in range(sents)]) for ref in (sl, tl))
    xw = (xwq_v, wsm.at[2, 0], wsm.at[2, 1], xsm_v.at[pl.ds(0, PAIR)], wsm.at[2, 2], xwo_v)
    c = norm(mid_v[1], xp_v[0:1, :], xp_v[1:2, :]).astype(BF16)
    low_v[1] = c
    mid_v[2] = mid_v[1] + mixture_fwd(c, mem_v[...], experts_of(xp_v, 2), xw, same_of(s_ends, t_ends), kept[1])

    groups = (
        (gff.at[1, 0], 1), (gff.at[1, 1], 1), (gx_v, None), (gff.at[0, 0], 0), (gff.at[0, 1], 0), (ge_v, 0), (gd_v, None),
    )
    live, waiting, state = {}, {}, {"stream": 0, "landed": 0, "mark": 0}
    steps_in_all = here.bits + scattered(n) + 3

    def done(i):
        pairs = {
            0: [(1, gff.at[1, 0], gff_out.at[pl.ds(0, FF)], 3)],
            1: [(1, gff.at[1, 1], gff_out.at[pl.ds(FF, FF)], 4)],
            2: [(None, gx_v, gx_out.at[pl.ds(0, 2 * D)], 5)],
            3: [(0, gff.at[0, 0], gff_out.at[pl.ds(0, FF)], 6)],
            4: [(0, gff.at[0, 1], gff_out.at[pl.ds(FF, FF)], 7)],
            5: [(0, ge_v, gat_out.at[pl.ds(0, 2 * D)], 8)],
            6: [(1, gd_v.at[pl.ds(0, 2 * D)], gat_out.at[pl.ds(0, 2 * D)], 9)]
            + [(l, gd_v.at[pl.ds(2 * D + l * NARROW, NARROW)], gat_out.at[pl.ds(2 * D, NARROW)], 10 + l) for l in range(2)]
            + [(None, gd_v.at[pl.ds(2 * D + 2 * NARROW, NARROW)], gx_out.at[pl.ds(2 * D, NARROW)], 12)],
        }
        for owner, src, dst, sem in pairs[i]:
            copy = pltpu.make_async_copy(src, dst, out_sem.at[sem])
            if owner is None:
                copy.start()
                finals.append(copy.wait)
            else:
                pl.when(sec == owner)(copy.start)
                finals.append(functools.partial(pl.when(sec == owner), copy.wait))

    def advance(k):
        i, steps = live[k]
        steps.pop(0)()
        if not steps:
            del live[k]
            if all(entry[0] != i for entry in live.values()):
                done(i)

    for i, (g, owner) in enumerate(groups):
        for first, rows, lands, order in streams_of(i, halves[i], n):
            k = state["stream"]
            steps = sum_steps(
                here, g, twin_in.at[i % 2], ring_in.at[pl.ds(state["landed"], lands)],
                sum_send.at[k], sum_recv.at[k], sum_free.at[k], halves[i], first, rows, order, owner,
            )
            waiting[k] = [i, steps]
            state["stream"] += 1
            state["landed"] += lands

    def begin(i):
        for k in [k for k in live if live[k][0] == i - 1 and len(live[k][1]) == steps_in_all - 1]:
            advance(k)
        for k in [k for k in waiting if waiting[k][0] == i]:
            live[k] = waiting.pop(k)
            advance(k)

    def mark():
        for k in MARKS[state["mark"]]:
            if k in live:
                advance(k)
        state["mark"] += 1

    def feed_start(l, middle):
        f = norm(middle, p(l, 2), p(l, 3))
        f_v[...] = f.astype(BF16)
        ft_v[...] = f.T.astype(BF16)
        dacc[...] = jnp.zeros_like(dacc)

    def feed_both(l, total, between):
        we, wr = we_v.at[l], wr_v.at[l]

        def step(j, carry):
            at = pl.multiple_of(j * CH, CH)
            part, to = lax.div(j, PART // CH), pl.multiple_of(lax.rem(j, PART // CH) * CH, CH)
            dy = cot_v[...]
            hidden, slope = gelu_both(expand_step(j, f_v, we, p_v.at[l]))
            hidden = hidden.astype(BF16)
            if total is not None:
                total[...] += dot(hidden, wr[pl.ds(at, CH), :])
            gff[l, part, pl.ds(pl.multiple_of(PART + to, CH), CH), :] = dot_tn(hidden, dy).astype(BF16)
            dpre = (dot_nt(dy, wr[pl.ds(at, CH), :]) * slope).astype(BF16)
            deb[l, pl.ds(j, 1), :] = jnp.sum(dpre.astype(F32), axis=0, keepdims=True)
            gff[l, part, pl.ds(to, CH), :] = dot(ft_v[...], dpre).astype(BF16)
            dacc[...] += dot_nt(dpre, we[:, pl.ds(at, CH)])
            for k, work in between.items():
                pl.when(j == k)(work)
            return carry

        lax.fori_loop(0, FF // CH, step, 0)

    def feed_end(l, middle):
        dend = cot_v[...].astype(F32)
        dmid, dgain, dbias = norm_back(dacc[...], middle, p(l, 2))
        return dmid + dend, [dgain, dbias, jnp.sum(dend, axis=0, keepdims=True)]

    swapped("p", "sm", "we", "wr")
    acc[...] = mid_v[2] + p(1, 4)
    feed_start(1, mid_v[2])
    feed_both(1, acc, {1: lambda: begin(0)})
    begin(1)
    out_v[...] = acc[...].astype(BF16)
    acc[...], feed_small = feed_end(1, mid_v[2])
    mark()
    own_rows = act_out.at[pl.ds(own_at, T)]
    out_near = pltpu.make_async_copy(out_v, own_rows, out_sem.at[2])
    out_away = remote(out_v, own_rows, out_send.at[0], out_recv.at[0])
    pl.when(sec == 1)(out_near.start)
    pl.when(sec == 0)(out_away.start)

    def narrow_tail(l, rows):
        at = 2 * D + l * NARROW + NARROW - 16
        gd_v[at : at + 16, :] = small_rows(rows).astype(BF16)

    dc, dmem = mixture_bwd(
        acc[...].astype(BF16), low_v[1], mem_v[...], experts_of(xp_v, 2), xw, same_of(s_ends, t_ends), kept[1],
        gx_v, 0, gd_v, 2 * D + 2 * NARROW, mark,
    )
    cot_v[...] = dmem.astype(BF16)
    dbefore, dgain, dbias = norm_back(dc, mid_v[1], xp_v[0:1, :])
    narrow_tail(2, [dgain, dbias])
    mid_v[2] = acc[...] + dbefore
    begin(2)
    mark()

    def self_fwd(l, with_out):
        x = x_v[l].astype(F32)
        a = norm(x, p(l, 0), p(l, 1)).astype(BF16)
        low_v[0] = a
        at = 9 + 2 * sec
        experts = [laid_out(p_v[l, pl.ds(at + r, 1), :]) for r in range(2)]
        ends = t_ends if l else s_ends
        allowed = same_of(ends, ends)
        allowed = allowed & earlier() if l else allowed
        out = mixture_fwd(a, a, experts, weights(l, sm_v.at[l]), allowed, kept[0], with_out)
        return x + out if with_out else None

    def self_back(l, grad, wide, feed_small):
        at = 9 + 2 * sec
        experts = [laid_out(p_v[l, pl.ds(at + r, 1), :]) for r in range(2)]
        ends = t_ends if l else s_ends
        allowed = same_of(ends, ends)
        allowed = allowed & earlier() if l else allowed
        da, ds = mixture_bwd(
            grad[...].astype(BF16), low_v[0], low_v[0], experts, weights(l, sm_v.at[l]), allowed, kept[0],
            wide, 0, gd_v, 2 * D + l * NARROW, mark,
        )
        dx, dgain, dbias = norm_back(da + ds, x_v[l].astype(F32), p(l, 0))
        mid_v[l] = grad[...] + dx
        narrow_tail(l, [dgain, dbias] + feed_small + [deb[l, i : i + 1, :] for i in range(FF // D)])

    swapped("wq", "wo", "x")
    lay_small(1 - sec, sm_v.at[1 - sec])
    mid_v[0] = self_fwd(0, True)
    mark()
    feed_start(0, mid_v[0])
    feed_both(0, None, {1: lambda: begin(3)})
    begin(4)
    acc[...], own_small = feed_end(0, mid_v[0])
    mark()
    self_back(0, acc, ge_v, own_small)
    begin(5)
    mark()

    self_fwd(1, False)
    mark()
    self_back(1, mid_v.at[2], gd_v, feed_small)
    at = 2 * D + 3 * NARROW
    gd_v[at:, :] = jnp.zeros((2 * halves[6] - at, D), BF16)
    begin(6)
    gin_rows = gin_out.at[pl.ds(own_at, T)]
    gin_near = pltpu.make_async_copy(mid_v.at[sec], gin_rows, out_sem.at[13])
    gin_away = remote(mid_v.at[1 - sec], gin_rows, out_send.at[1], out_recv.at[1])
    gin_near.start()
    gin_away.start()
    mark()
    mark()
    while live:
        for k in list(live):
            advance(k)
    for wait in finals:
        wait()
    gin_near.wait()
    gin_away.wait()

    @pl.when(sec == 0)
    def _():
        out_away.wait_send()
        for copy in memory_out:
            copy.wait()

    @pl.when(sec == 1)
    def _():
        out_away.wait_recv()
        out_near.wait()


def widen(act, gin, gff, gat, gx, *refs):
    outs, (act_v, gin_v, gff_v, gat_v, gx_v, ex_v, re_v, mats, in_sem, out_sem) = refs[:-10], refs[-10:]
    act_out, gin_out, expand, reduce, q, o, xq, xo = outs[:8]
    smalls = outs[8:]
    loads, at = [], 0
    for ref, dst in ((gff, gff_v), (gat, gat_v), (gx, gx_v)):
        for first in range(0, ref.shape[0], D):
            rows = pl.ds(first, min(D, ref.shape[0] - first))
            loads.append(pltpu.make_async_copy(ref.at[rows], dst.at[rows], in_sem.at[at]))
            loads[-1].start()
            at += 1
    passing = [
        pltpu.make_async_copy(a, b, in_sem.at[at + i]) for i, (a, b) in enumerate(((act, act_v), (gin, gin_v)))
    ]
    for copy in passing:
        copy.start()
    stores = []

    def store(src, dst):
        stores.append(pltpu.make_async_copy(src, dst, out_sem.at[len(stores)]))
        stores[-1].start()

    blocks = PART // D
    for i in range(2 * FF // D):
        loads[i].wait()
        part, kind, block = i // (2 * blocks), (i // blocks) % 2, i % blocks
        col = part * PART + block * D
        value = gff_v[i * D : (i + 1) * D, :].astype(F32)
        if kind == 0:
            ex_v[:, col : col + D] = value
            store(ex_v.at[:, pl.ds(col, D)], expand.at[:, pl.ds(col, D)])
        else:
            re_v[col : col + D, :] = value
            store(re_v.at[pl.ds(col, D)], reduce.at[pl.ds(col, D)])
    i = 2 * FF // D
    for m, (src, row, dst) in enumerate(((gat_v, 0, q), (gat_v, D, o), (gx_v, 0, xq), (gx_v, D, xo))):
        loads[i + m + m // 2].wait()
        mats[m] = src[row : row + D, :].astype(F32)
        store(mats.at[m], dst)
    for k, load in enumerate((loads[i + 2], loads[i + 5])):
        load.wait()
        src = (gat_v, gx_v)[k]
        ks, vs, rs = smalls[:3] if k == 0 else smalls[9:12]
        at = 2 * D
        ks[...] = src[at : at + 64, :].astype(F32)
        vs[...] = src[at + 64 : at + PAIR, :].astype(F32)
        rs[...] = src[at + PAIR : at + PAIR + 16, :].astype(F32)[0:8]
        tail = src[at + PAIR + 16 : at + NARROW, :].astype(F32)
        if k == 0:
            for j in range(5):
                smalls[3 + j][...] = tail[j : j + 1]
            for j in range(FF // D):
                smalls[8][:, j * D : (j + 1) * D] = tail[5 + j : 6 + j]
        else:
            for j in range(2):
                smalls[12 + j][...] = tail[j : j + 1]
    for copy, src, dst in zip(passing, (act_v, gin_v), (act_out, gin_out)):
        copy.wait()
        store(src, dst)
    for copy in stores:
        copy.wait()


def body(n, *arrays):
    (
        embeddings, cotangent, source_lengths, target_lengths, self_routes, cross_routes,
        attend_gain, attend_bias, self_router, query_weight, key_weight, value_weight, output_weight,
        feed_gain, feed_bias, expand_weight, expand_bias, reduce_weight, reduce_bias,
        cross_gain, cross_bias, cross_router, cross_query, cross_key, cross_value, cross_output,
    ) = arrays
    row_count = embeddings.shape[1]
    sents = source_lengths.shape[1]
    part = up(PART, n)
    halves = (part, part, up(D, n), part, part, up(D, n), up((2 * D + 3 * NARROW + 1) // 2, n))
    cut = [stream for i, half in enumerate(halves) for stream in streams_of(i, half, n)]
    streams, lands = len(cut), sum(stream[2] for stream in cut)
    steps = n.bit_length() - 1 + scattered(n) + 2
    S, V, DMA = jax.ShapeDtypeStruct, pltpu.VMEM, pltpu.SemaphoreType.DMA
    hbm, smem = pl.BlockSpec(memory_space=pl.ANY), pl.BlockSpec(memory_space=pltpu.SMEM)
    vmem = pl.BlockSpec(memory_space=pltpu.VMEM)
    rows = 2 * D + NARROW
    act, gin, gff, gat, gx = pl.pallas_call(
        functools.partial(fused, n, halves, sents),
        in_specs=[smem] * 2 + [vmem] * 16 + [hbm] * 8,
        out_specs=[hbm] * 5,
        out_shape=[
            S((row_count, D), BF16), S((row_count, D), F32),
            S((2 * FF, D), BF16), S((rows, D), BF16), S((rows, D), BF16),
        ],
        scratch_shapes=[
            V((3, T, D), BF16), V((2, 16, D), F32), V((16, D), F32), V((2, NARROW, D), BF16), V((NARROW, D), BF16),
            V((2, D, D), BF16), V((2, D, D), BF16), V((2, D, FF), BF16), V((2, FF, D), BF16),
            V((T, D), BF16), V((D, D), BF16), V((D, D), BF16),
            V((3, 3, PAIR, D), BF16), [[V(s, t) for _, s, t in KEPT] for _ in range(2)],
            V((2, T, D), BF16), V((3, T, D), F32), V((T, D), BF16), V((T, D), BF16), V((T, D), BF16), V((D, T), BF16),
            V((2, T, D), F32), V((2, 8, D), F32), V((T, D), BF16),
            V((2, PARTS, 2 * part, D), BF16), *(V((2 * halves[i], D), BF16) for i in (2, 5, 6)),
            V((2, max(halves), D), BF16), V((lands, D), BF16), DMA((streams,)), DMA((streams, steps)),
            pltpu.SemaphoreType.REGULAR((streams, 1 + scattered(n))),
            DMA((9,)), DMA((9,)), DMA((9,)), DMA((14,)), DMA((2,)), DMA((2,)),
        ],
        compiler_params=pltpu.CompilerParams(
            collective_id=0, has_side_effects=True, vmem_limit_bytes=(63 << 20) + (900 << 10)
        ),
    )(
        source_lengths, target_lengths, self_routes[0].T, cross_routes.T,
        attend_gain, attend_bias, feed_gain, feed_bias, reduce_bias, expand_bias,
        key_weight[0].T, value_weight[0].T, self_router[0].T,
        cross_gain[None], cross_bias[None], cross_key.T, cross_value.T, cross_router.T,
        embeddings[0], cotangent, query_weight[0], output_weight[0], expand_weight[0], reduce_weight[0],
        cross_query, cross_output,
    )
    wide = [(row_count, D), (row_count, D), (D, FF), (FF, D)] + [(D, D)] * 4
    narrow = [(64, D), (64, D), (8, D)] + [(1, D)] * 5 + [(1, FF)] + [(64, D), (64, D), (8, D)] + [(1, D)] * 2
    out = pl.pallas_call(
        widen,
        in_specs=[hbm] * 5,
        out_specs=[hbm] * len(wide) + [vmem] * len(narrow),
        out_shape=[S(s, BF16 if i == 0 else F32) for i, s in enumerate(wide + narrow)],
        scratch_shapes=[
            V((row_count, D), BF16), V((row_count, D), F32), V((2 * FF, D), BF16), V((rows, D), BF16), V((rows, D), BF16),
            V((D, FF), F32), V((FF, D), F32), V((4, D, D), F32), DMA((2 * FF // D + 8,)), DMA((2 * FF // D + 6,)),
        ],
        compiler_params=pltpu.CompilerParams(vmem_limit_bytes=(63 << 20) + (900 << 10)),
    )(act, gin, gff, gat, gx)
    act, gin, expand, reduce, q, o, xq, xo = out[:8]
    k, v, r, gains, biases, fgain, fbias, rbias, ebias, xk, xv, xr, xgain, xbias = out[8:]
    return (
        act[None], gin[None], gains, biases, r.T[None], q[None], k.T[None], v.T[None], o[None],
        fgain, fbias, expand[None], ebias, reduce[None], rbias,
        xgain[0], xbias[0], xr.T, xq, xk.T, xv.T, xo,
    )


def solution(mesh):
    n = mesh.shape["dp"]
    stacked, rows = P("section", None), P("dp", None)
    matrix, both = P("section", None, None), P("section", "dp", None)
    params = (
        stacked, stacked, matrix, matrix, matrix, matrix, matrix, stacked, stacked, matrix, stacked, matrix, stacked,
    ) + (P(),) * 7
    return jax.shard_map(
        functools.partial(body, n),
        mesh=mesh,
        in_specs=(both, rows, rows, rows, both, rows) + params,
        out_specs=(both, both) + params,
        check_vma=False,
    )
```

```python
import functools
import math

import jax
import jax.numpy as jnp
from jax import lax
from jax.experimental import pallas as pl
from jax.experimental.pallas import tpu as pltpu
from jax.sharding import PartitionSpec as P

EPSILON = 1e-05
SCORE_SCALE = 0.125
MASKED_SCORE = -1000000000.0
F32 = jnp.float32
BF16 = jnp.bfloat16
T = 512
D = 512
FF = 2048
PAIR = 128
CH = 512
PARTS = 2
PART = FF // PARTS
NARROW = 160
MESH = pl.DeviceIdType.MESH


def dot(a, b):
    return lax.dot_general(a, b, (((1,), (0,)), ((), ())), preferred_element_type=F32)


def dot_nt(a, b):
    return lax.dot_general(a, b, (((1,), (1,)), ((), ())), preferred_element_type=F32)


def dot_tn(a, b):
    return lax.dot_general(a, b, (((0,), (0,)), ((), ())), preferred_element_type=F32)


def iota(shape, axis):
    return lax.broadcasted_iota(jnp.int32, shape, axis)


def norm_parts(v):
    centred = v - jnp.mean(v, axis=-1, keepdims=True)
    spread = jnp.mean(centred * centred, axis=-1, keepdims=True)
    return centred, lax.rsqrt(spread + EPSILON)


def norm(v, gain, bias):
    centred, scale = norm_parts(v)
    return centred * scale * gain + bias


def norm_back(dn, v, gain):
    centred, scale = norm_parts(v)
    unit = centred * scale
    dgain = jnp.sum(dn * unit, axis=0, keepdims=True)
    dbias = jnp.sum(dn, axis=0, keepdims=True)
    dunit = dn * gain
    first = jnp.mean(dunit, axis=-1, keepdims=True)
    second = jnp.mean(dunit * unit, axis=-1, keepdims=True)
    return scale * (dunit - first - unit * second), dgain, dbias


def ids_of(ends, shape, axis):
    places = iota(shape, axis)
    total = jnp.zeros(shape, jnp.int32)
    for end in ends:
        total = total + (places >= end).astype(jnp.int32)
    return total


def ends_of(lengths):
    ends, total = [], jnp.int32(0)
    for length in lengths:
        total = total + length
        ends.append(total)
    return ends


def same_of(key_ends, query_ends):
    return ids_of(key_ends, (T, 1), 0) == ids_of(query_ends, (1, T), 1)


def earlier():
    return iota((T, T), 0) <= iota((T, T), 1)


def chosen(expert, block):
    return expert == (iota((T, PAIR), 1) // 64 + 2 * block).astype(F32)


def laid_out(row):
    return jnp.broadcast_to(row, (PAIR, T)).T


def mixture_fwd(a, s, experts, w, allowed, kept, with_out=True):
    wq, wk2, wv2, wkv, wr2, wo = w
    q = dot(a, wq[...])
    logits = dot_nt(a, wr2[...])
    kk = dot_nt(s, wk2[...]).astype(BF16)
    vv = dot_nt(s, wv2[...]).astype(BF16)
    kept["kk"][...] = kk
    kept["vv"][...] = vv
    lanes = iota((T, PAIR), 1).astype(F32)
    raised = [
        jnp.exp(jnp.sum(jnp.where(lanes == e, logits, 0.0), axis=-1, keepdims=True))
        for e in experts
    ]
    total = raised[0] + raised[1]
    gated = [jnp.zeros((T, PAIR), F32) for _ in range(4)]
    for r in range(2):
        gate = raised[r] / total
        kept["gate"][r] = jnp.broadcast_to(gate, (T, PAIR))
        qs = jnp.zeros((T, PAIR), F32)
        for b in range(4):
            qs = jnp.where(chosen(experts[r], b), q[:, b * PAIR : (b + 1) * PAIR], qs)
        qs = qs.astype(BF16)
        kept["qs"][r] = qs
        scores = jnp.where(allowed, dot_nt(kk, qs) * SCORE_SCALE, MASKED_SCORE)
        top = jnp.max(scores, axis=0, keepdims=True)
        p = jnp.exp(scores - top)
        inverse = 1.0 / jnp.sum(p, axis=0, keepdims=True)
        kept["top"][r : r + 1] = top
        kept["inv"][r : r + 1] = inverse
        chance = (p * inverse).astype(BF16)
        mixed = dot_tn(vv, chance).T
        kept["mixed"][r] = mixed
        weighted = gate * mixed
        for b in range(4):
            gated[b] = jnp.where(chosen(experts[r], b), weighted, gated[b])
    for b in range(4):
        kept["gated"][:, b * PAIR : (b + 1) * PAIR] = gated[b].astype(BF16)
    if with_out:
        return dot(kept["gated"][...], wo[...])


def mixture_bwd(dy, a, s, experts, w, allowed, kept, wide, base, narrow, nbase, mark):
    wq, wk2, wv2, wkv, wr2, wo = w
    wide[base + D : base + 2 * D, :] = dot_tn(kept["gated"][...], dy).astype(BF16)
    dgated = dot_nt(dy, wo[...]).astype(BF16).astype(F32)
    kk, vv = kept["kk"][...], kept["vv"][...]
    lanes = iota((T, PAIR), 1)
    dkk = jnp.zeros((T, PAIR), F32)
    dvv = jnp.zeros((T, PAIR), F32)
    dgates, gates, dqs = [], [], []
    for r in range(2):
        own = jnp.zeros((T, PAIR), F32)
        for b in range(4):
            own = jnp.where(chosen(experts[r], b), dgated[:, b * PAIR : (b + 1) * PAIR], own)
        gate = kept["gate"][r]
        gates.append(gate)
        dgates.append(jnp.sum(own * kept["mixed"][r], axis=-1, keepdims=True))
        dmixed = (gate * own).astype(BF16)
        qs = kept["qs"][r]
        scores = jnp.where(allowed, dot_nt(kk, qs) * SCORE_SCALE, MASKED_SCORE)
        p = jnp.exp(scores - kept["top"][r : r + 1]) * kept["inv"][r : r + 1]
        dp = dot_nt(vv, dmixed)
        both = jnp.sum(p * dp, axis=0, keepdims=True)
        ds = (p * (dp - both)).astype(BF16)
        dkk = dkk + dot(ds, qs)
        dvv = dvv + dot(p.astype(BF16), dmixed)
        dqs.append((dot_tn(kk, ds) * SCORE_SCALE).T)
        mark()
    dq = []
    for b in range(4):
        part = jnp.zeros((T, PAIR), F32)
        for r in range(2):
            part = jnp.where(chosen(experts[r], b), dqs[r], part)
        dq.append(part.astype(BF16))
    dq = jnp.concatenate(dq, axis=1)
    dk = (dkk + pltpu.roll(dkk, 64, 1)) * SCORE_SCALE
    dv = dvv + pltpu.roll(dvv, 64, 1)
    dkv = jnp.where(lanes < 64, dk, dv).astype(BF16)
    mean = gates[0] * dgates[0] + gates[1] * dgates[1]
    dl = jnp.zeros((T, PAIR), F32)
    for r in range(2):
        dl = jnp.where(((lanes % 8).astype(F32) == experts[r]) & (lanes < 16), gates[r] * (dgates[r] - mean), dl)
    high = dl.astype(BF16).astype(F32)
    dl = jnp.where(lanes < 8, high, dl - high).astype(BF16)
    wide[base : base + D, :] = dot_tn(a, dq).astype(BF16)
    narrow[nbase : nbase + PAIR, :] = dot_tn(dkv, s).astype(BF16)
    dwr = dot_tn(dl, a)
    dwr = dwr[0:8] + dwr[8:16]
    narrow[nbase + PAIR : nbase + PAIR + 16, :] = jnp.concatenate([dwr, jnp.zeros((8, D), F32)], axis=0).astype(BF16)
    da = dot_nt(dq, wq[...]) + dot(dl, wr2[...])
    ds = dot(dkv, wkv[...])
    return da, ds


C0, C1 = 0.7978845608028654, 0.044715


def gelu(pre):
    half = 0.5 * jnp.tanh(C0 * (pre + C1 * pre * pre * pre)) + 0.5
    return pre * half


def gelu_both(pre):
    square = pre * pre
    t = jnp.tanh(C0 * pre * (1.0 + C1 * square))
    half = 0.5 * t + 0.5
    slope = half + 0.5 * pre * (1.0 - t * t) * (C0 * (1.0 + 3.0 * C1 * square))
    return pre * half, slope


def expand_step(j, f, we, p):
    at = pl.multiple_of(j * CH, CH)
    return dot(f[...], we[:, pl.ds(at, CH)]) + p[pl.ds(5 + j, 1), :]


def feed_fwd(f, acc, we, p, wr, ready):
    def step(j, carry):
        ready(j)
        hidden = gelu(expand_step(j, f, we, p)).astype(BF16)
        acc[...] += dot(hidden, wr[pl.ds(pl.multiple_of(j * CH, CH), CH), :])
        return carry

    lax.fori_loop(0, FF // CH, step, 0)


def small_rows(rows, count=16):
    places = iota((count, D), 0)
    out = jnp.zeros((count, D), F32)
    for i, row in enumerate(rows):
        out = jnp.where(places == i, row, out)
    return out


KEPT = (
    ("kk", (T, PAIR), BF16),
    ("vv", (T, PAIR), BF16),
    ("gate", (2, T, PAIR), F32),
    ("qs", (2, T, PAIR), BF16),
    ("top", (8, T), F32),
    ("inv", (8, T), F32),
    ("mixed", (2, T, PAIR), F32),
    ("gated", (T, D), BF16),
)


class Here:
    def __init__(self, n):
        self.bits = n.bit_length() - 1
        self.sec = lax.axis_index("section")
        self.rank = lax.axis_index("dp")

    def side(self, b):
        return lax.rem(self.rank // (1 << b), 2)

    def partner(self, b):
        return (self.sec, self.rank + (1 - 2 * self.side(b)) * (1 << b))

    def twin(self):
        return (1 - self.sec, self.rank)


def scattered(n):
    return min(4, n.bit_length() - 1)


def up(rows, n):
    unit = 16 << scattered(n)
    return -(-rows // unit) * unit


PLAN = (
    ((1, (1, 0, 2, 3)), (2, (1, 0, 2, 3)), (1, (0, 1, 2, 3))),
    ((1, (2, 0, 1, 3)), (1, (0, 1, 2, 3)), (2, (0, 1, 2, 3))),
    ((1, (2, 1, 0, 3)), (1, (1, 2, 0, 3))),
    ((2, (2, 0, 1, 3)), (1, (1, 0, 2, 3)), (1, (1, 0, 2, 3))),
    ((1, (2, 0, 1, 3)), (1, (0, 1, 2, 3)), (2, (0, 1, 2, 3))),
    ((1, (1, 0, 2, 3)), (1, (2, 0, 1, 3))),
    ((1, (1, 0, 2, 3)), (1, (1, 0, 2, 3)), (1, (0, 1, 2, 3))),
)
MARKS = (
    (),
    (),
    (),
    (0, 2),
    (1, 3, 2, 4, 5, 6, 0, 7),
    (11, 12, 13),
    (9,),
    (1, 8, 10, 2, 3, 0, 4),
    (7, 12, 5),
    (11, 6, 3, 1, 2),
    (0, 4, 14, 15, 13, 12, 5, 9),
    (3,),
    (8, 1, 2, 10, 0, 7, 4, 11),
    (
        14, 6, 15, 12, 16, 17, 18, 13, 5, 9, 3, 8, 2, 11, 1, 10, 14, 0, 7, 15, 4, 6, 16, 12,
        13, 18, 5, 9, 17, 0, 1, 3, 8, 16, 11, 14, 2, 10, 15, 4, 7, 17, 6, 18, 12, 5, 13, 1,
        9, 0, 16, 3, 8, 4, 11, 17, 0, 14, 10, 18, 2, 15, 5, 12, 7, 6, 9, 13, 2, 16, 4, 3,
        17, 1, 4, 10, 14, 18, 8, 3, 15, 11, 7, 1, 12, 5, 13, 16, 6, 9, 14, 17, 15, 18, 5, 10,
        16, 7, 8, 6, 7, 11, 17, 13, 18, 6, 12, 9, 14, 12, 9, 15, 10, 8, 16, 18, 10, 17, 8, 11,
        14, 11, 15, 14, 16, 13, 15, 16, 17, 13, 18, 17, 18,
    ),
)


def streams_of(group, half, n):
    bits = n.bit_length() - 1
    shares = sum(share for share, _ in PLAN[group])
    out, at = [], 0
    for share, order in PLAN[group]:
        rows = half * share // shares
        piece = rows >> scattered(n)
        lands = rows - piece + (bits - scattered(n)) * piece
        out.append((at, rows, lands, [b for b in order if b < bits] + list(range(4, bits))))
        at += rows
    return out


def add_rows(dst, at, src, start, rows):
    block = math.gcd(rows, 128)

    def step(i, carry):
        to = pl.ds(pl.multiple_of(at + i * block, 16), block)
        dst[to, :] = dst[to, :] + src[pl.ds(pl.multiple_of(start + i * block, 16), block), :]
        return carry

    lax.fori_loop(0, rows // block, step, 0)


def sum_steps(here, g, twin_in, ring_in, send, recv, free, half, first, rows, order, owner):
    def remote(i, src, dst, device):
        return pltpu.make_async_remote_copy(
            src_ref=src, dst_ref=dst, send_sem=send, recv_sem=recv.at[i],
            device_id=device, device_id_type=MESH,
        )

    def rows_at(at, count):
        return g.at[pl.ds(pl.multiple_of(at, 16), count)]

    def signal(i, device):
        pl.semaphore_signal(free.at[i], inc=1, device_id=device, device_id_type=MESH)

    def summed(copy, credit, device, at, source, start, length):
        def end():
            copy.wait()
            if credit is not None:
                signal(credit, device)
            add_rows(g, at, source, start, length)

        return end

    def after(credit, copy):
        def start():
            pl.semaphore_wait(free.at[credit], 1)
            copy.start()

        return start

    mine = here.sec * half + first
    other = (1 - here.sec) * half + first
    copies = 0
    copy = remote(copies, rows_at(other, rows), twin_in.at[pl.ds(first, rows)], here.twin())
    moves = [(copy.start, summed(copy, 0, here.twin(), mine, twin_in, first, rows))]
    at, length, landing, trail = mine, rows, 0, []
    for step, b in enumerate(order):
        copies += 1
        partner = here.partner(b)
        if step >= 4:
            copy = remote(copies, rows_at(at, length), ring_in.at[pl.ds(landing, length)], partner)
            moves.append((copy.start, summed(copy, None, partner, at, ring_in, landing, length)))
            landing += length
            continue
        length //= 2
        side = here.side(b)
        keep, give = at + side * length, at + (1 - side) * length
        copy = remote(copies, rows_at(give, length), ring_in.at[pl.ds(landing, length)], partner)
        moves.append((copy.start, summed(copy, 1 + step, partner, keep, ring_in, landing, length)))
        trail.append((b, at, length))
        at, landing = keep, landing + length
    for step, (b, before, length) in reversed(list(enumerate(trail))):
        copies += 1
        copy = remote(copies, rows_at(at, length), rows_at(at, length), here.partner(b))
        moves.append((after(1 + step, copy), copy.wait))
        at = before
    copies += 1
    copy = remote(copies, rows_at(mine, rows), rows_at(mine, rows), here.twin())
    if owner is None:
        moves.append((after(0, copy), copy.wait))
    else:
        gives = here.sec != owner

        def start():
            pl.semaphore_wait(free.at[0], 1)
            pl.when(gives)(copy.start)

        def end():
            pl.when(gives)(copy.wait_send)
            pl.when(jnp.logical_not(gives))(copy.wait_recv)

        moves.append((start, end))
    ends = [end for _, end in moves]
    starts = [start for start, _ in moves[1:]]

    def both(end, start):
        def step():
            end()
            start()

        return step

    return [moves[0][0]] + [both(end, start) for end, start in zip(ends, starts)] + [ends[-1]]


def fused(n, halves, sents, *refs):
    (
        sl, tl, routes, xroutes, ag, ab, fg, fb, rb, eb, wk, wv, wrt, cg, cb, xwk, xwv, xwrt,
        emb, cot, wq, wo, we, wr, xwq, xwo,
        act_out, gin_out, gff_out, gat_out, gx_out,
        x_v, p_v, xp_v, sm_v, xsm_v, wq_v, wo_v, we_v, wr_v, cot_v, xwq_v, xwo_v,
        wsm, kept_refs, low_v, mid_v, mem_v, f_v, ft_v, totals, deb, out_v,
        gff, gx_v, ge_v, gd_v, twin_in, ring_in, sum_send, sum_recv, sum_free,
        own_sem, in_send, in_recv, out_sem, out_send, out_recv,
    ) = refs
    here = Here(n)
    sec = here.sec
    acc, dacc = totals.at[0], totals.at[1]
    barrier = pltpu.get_barrier_semaphore()
    pl.semaphore_signal(barrier, inc=1, device_id=here.twin(), device_id_type=MESH)
    for b in range(here.bits):
        pl.semaphore_signal(barrier, inc=1, device_id=here.partner(b), device_id_type=MESH)

    def slot(ref, which):
        return ref.at[pl.ds(pl.multiple_of(which * T, T), T)]

    def remote(src, dst, send, recv):
        return pltpu.make_async_remote_copy(
            src_ref=src, dst_ref=dst, send_sem=send, recv_sem=recv, device_id=here.twin(), device_id_type=MESH
        )

    local = {}
    for i, (name, src, dst) in enumerate((
        ("x_oth", slot(emb, 1 - sec), x_v.at[2]), ("x", slot(emb, sec), x_v.at[sec]), ("wq", wq, wq_v.at[sec]),
        ("wo", wo, wo_v.at[sec]), ("we", we, we_v.at[sec]), ("wr", wr, wr_v.at[sec]),
        ("xwq", xwq, xwq_v), ("xwo", xwo, xwo_v), ("cot", slot(cot, sec), cot_v),
    )):
        local[name] = pltpu.make_async_copy(src, dst, own_sem.at[i])
        local[name].start()

    def need(*names):
        for name in names:
            local[name].wait()

    own_at = pl.multiple_of(sec * T, T)
    p_v[sec] = small_rows(
        [ref[...] for ref in (ag, ab, fg, fb, rb)]
        + [eb[:, i * D : (i + 1) * D] for i in range(FF // D)]
        + [routes[r : r + 1, m * T : (m + 1) * T].astype(F32) for m in range(2) for r in range(2)]
    )
    xp_v[...] = small_rows(
        [cg[...], cb[...]] + [xroutes[r : r + 1, pl.ds(own_at, T)].astype(F32) for r in range(2)]
    )

    def pack(wk, wv, wrt):
        router = wrt[...].astype(F32)
        tail = jnp.concatenate([router, router, jnp.zeros((16, D), F32)], axis=0).astype(BF16)
        return jnp.concatenate([wk[...], wv[...], tail], axis=0)

    sm_v[sec] = pack(wk, wv, wrt)
    xsm_v[...] = pack(xwk, xwv, xwrt)

    def lay_small(l, ref):
        for i in range(2):
            half = ref[64 * i : 64 * i + 64]
            wsm[l, i] = jnp.concatenate([half, half], axis=0)
        wsm[l, 2] = jnp.concatenate([ref[128:144], jnp.zeros((112, D), BF16)], axis=0)

    def weights(l, small):
        return (
            wq_v.at[l], wsm.at[l, 0], wsm.at[l, 1], small.at[pl.ds(0, PAIR)], wsm.at[l, 2], wo_v.at[l],
        )

    def p(l, i):
        return p_v[l, i : i + 1, :]

    def experts_of(ref, first):
        return [laid_out(ref[first + r : first + r + 1, :]) for r in range(2)]

    kept = [dict(zip([k[0] for k in KEPT], k)) for k in kept_refs]

    lay_small(sec, sm_v.at[sec])

    def own_middle(i, carry):
        row = jnp.where(i == 0, 1 - sec, sec)
        ends = ends_of([jnp.where(sec == 0, sl[row, i], tl[row, i]) for i in range(sents)])
        allowed = same_of(ends, ends) & (earlier() | (sec == 0))
        x = x_v[jnp.where(i == 0, 2, sec)].astype(F32)
        a = norm(x, p(sec, 0), p(sec, 1)).astype(BF16)
        at = 9 + 2 * row
        experts = [laid_out(p_v[sec, pl.ds(at + r, 1), :]) for r in range(2)]
        totals[1 - i] = x + mixture_fwd(a, a, experts, weights(sec, sm_v.at[sec]), allowed, kept[0])

        @pl.when(i == 0)
        def _():
            pl.semaphore_wait(barrier, here.bits + 1)
            for name in ("middle", "p", "sm"):
                swaps[name].start()
            for j in range(FF // CH):
                for copy in feed_swaps(j):
                    copy.start()
            for name in ("wq", "wo", "x"):
                swaps[name].start()

        return carry

    swaps = {}
    for i, (name, src, dst) in enumerate((
        ("p", p_v.at[sec], p_v), ("sm", sm_v.at[sec], sm_v), ("wq", wq, wq_v), ("wo", wo, wo_v),
        ("x", slot(emb, 1 - sec), x_v), ("middle", dacc, mid_v),
    )):
        swaps[name] = remote(src, dst.at[sec], in_send.at[i], in_recv.at[i])

    def feed_swaps(j):
        rows = pl.ds(pl.multiple_of(j * CH, CH), CH)
        first = len(swaps) + 2 * j
        return (
            remote(we.at[:, rows], we_v.at[sec, :, rows], in_send.at[first], in_recv.at[first]),
            remote(wr.at[rows], wr_v.at[sec, rows], in_send.at[first + 1], in_recv.at[first + 1]),
        )

    def swapped(*names):
        for name in names:
            swaps[name].wait()

    need("x_oth", "x", "wq", "wo")
    lax.fori_loop(0, 2, own_middle, 0)
    need("we", "wr")
    mid_v[sec] = acc[...]
    swapped("middle", "p", "sm")
    f_v[...] = norm(mid_v[0], p(0, 2), p(0, 3)).astype(BF16)
    acc[...] = mid_v[0] + p(0, 4)

    def feed_ready(j):
        for copy in feed_swaps(j):
            copy.wait()

    feed_fwd(f_v, acc, we_v.at[0], p_v.at[0], wr_v.at[0], feed_ready)
    mem_v[...] = acc[...].astype(BF16)
    lay_small(1 - sec, sm_v.at[1 - sec])
    need("xwq", "xwo", "cot")
    lay_small(2, xsm_v)
    finals = []

    def hand_out(start, end):
        start()
        finals.append(end)

    own_rows = act_out.at[pl.ds(own_at, T)]
    rows_out = []
    for i, ref in enumerate((mem_v, out_v)):
        near = pltpu.make_async_copy(ref, own_rows, out_sem.at[i])
        away = remote(ref, own_rows, out_send.at[i], out_recv.at[i])
        rows_out.append((near, away))

    def rows_start(i):
        pl.when(sec == i)(rows_out[i][0].start)
        pl.when(sec != i)(rows_out[i][1].start)

    def rows_end(i):
        pl.when(sec != i)(rows_out[i][1].wait_send)

        @pl.when(sec == i)
        def _():
            rows_out[i][0].wait()
            rows_out[i][1].wait_recv()

    rows_start(0)

    s_ends, t_ends = (ends_of([ref[sec, i] for i in range(sents)]) for ref in (sl, tl))
    xw = (xwq_v, wsm.at[2, 0], wsm.at[2, 1], xsm_v.at[pl.ds(0, PAIR)], wsm.at[2, 2], xwo_v)
    c = norm(mid_v[1], xp_v[0:1, :], xp_v[1:2, :]).astype(BF16)
    low_v[1] = c
    mid_v[2] = mid_v[1] + mixture_fwd(c, mem_v[...], experts_of(xp_v, 2), xw, same_of(s_ends, t_ends), kept[1])

    groups = (
        (gff.at[1, 0], 1), (gff.at[1, 1], 1), (gx_v, None), (gff.at[0, 0], 0), (gff.at[0, 1], 0), (ge_v, 0), (gd_v, None),
    )
    live, waiting, state = {}, {}, {"stream": 0, "landed": 0, "mark": 0}
    steps_in_all = here.bits + scattered(n) + 3

    def done(i):
        pairs = {
            0: [(1, gff.at[1, 0], gff_out.at[pl.ds(0, FF)], 3)],
            1: [(1, gff.at[1, 1], gff_out.at[pl.ds(FF, FF)], 4)],
            2: [(None, gx_v, gx_out.at[pl.ds(0, 2 * D)], 5)],
            3: [(0, gff.at[0, 0], gff_out.at[pl.ds(0, FF)], 6)],
            4: [(0, gff.at[0, 1], gff_out.at[pl.ds(FF, FF)], 7)],
            5: [(0, ge_v, gat_out.at[pl.ds(0, 2 * D)], 8)],
            6: [(1, gd_v.at[pl.ds(0, 2 * D)], gat_out.at[pl.ds(0, 2 * D)], 9)]
            + [(l, gd_v.at[pl.ds(2 * D + l * NARROW, NARROW)], gat_out.at[pl.ds(2 * D, NARROW)], 10 + l) for l in range(2)]
            + [(None, gd_v.at[pl.ds(2 * D + 2 * NARROW, NARROW)], gx_out.at[pl.ds(2 * D, NARROW)], 12)],
        }
        for owner, src, dst, sem in pairs[i]:
            copy = pltpu.make_async_copy(src, dst, out_sem.at[sem])
            if owner is None:
                copy.start()
                finals.append(copy.wait)
            else:
                pl.when(sec == owner)(copy.start)
                finals.append(functools.partial(pl.when(sec == owner), copy.wait))

    def advance(k):
        i, steps = live[k]
        steps.pop(0)()
        if not steps:
            del live[k]
            if all(entry[0] != i for entry in live.values()):
                done(i)

    for i, (g, owner) in enumerate(groups):
        for first, rows, lands, order in streams_of(i, halves[i], n):
            k = state["stream"]
            steps = sum_steps(
                here, g, twin_in.at[i % 2], ring_in.at[pl.ds(state["landed"], lands)],
                sum_send.at[k], sum_recv.at[k], sum_free.at[k], halves[i], first, rows, order, owner,
            )
            waiting[k] = [i, steps]
            state["stream"] += 1
            state["landed"] += lands

    def begin(i):
        for k in [k for k in live if live[k][0] == i - 1 and len(live[k][1]) == steps_in_all - 1]:
            advance(k)
        for k in [k for k in waiting if waiting[k][0] == i]:
            live[k] = waiting.pop(k)
            advance(k)

    def mark():
        for k in MARKS[state["mark"]]:
            if k in live:
                advance(k)
        state["mark"] += 1

    def feed_start(l, middle):
        f = norm(middle, p(l, 2), p(l, 3))
        f_v[...] = f.astype(BF16)
        ft_v[...] = f.T.astype(BF16)
        dacc[...] = jnp.zeros_like(dacc)

    def feed_both(l, total, between):
        we, wr = we_v.at[l], wr_v.at[l]

        def step(j, carry):
            at = pl.multiple_of(j * CH, CH)
            part, to = lax.div(j, PART // CH), pl.multiple_of(lax.rem(j, PART // CH) * CH, CH)
            dy = cot_v[...]
            hidden, slope = gelu_both(expand_step(j, f_v, we, p_v.at[l]))
            hidden = hidden.astype(BF16)
            if total is not None:
                total[...] += dot(hidden, wr[pl.ds(at, CH), :])
            gff[l, part, pl.ds(pl.multiple_of(PART + to, CH), CH), :] = dot_tn(hidden, dy).astype(BF16)
            dpre = (dot_nt(dy, wr[pl.ds(at, CH), :]) * slope).astype(BF16)
            deb[l, pl.ds(j, 1), :] = jnp.sum(dpre.astype(F32), axis=0, keepdims=True)
            gff[l, part, pl.ds(to, CH), :] = dot(ft_v[...], dpre).astype(BF16)
            dacc[...] += dot_nt(dpre, we[:, pl.ds(at, CH)])
            for k, work in between.items():
                pl.when(j == k)(work)
            return carry

        lax.fori_loop(0, FF // CH, step, 0)

    def feed_end(l, middle):
        dend = cot_v[...].astype(F32)
        dmid, dgain, dbias = norm_back(dacc[...], middle, p(l, 2))
        return dmid + dend, [dgain, dbias, jnp.sum(dend, axis=0, keepdims=True)]

    acc[...] = mid_v[2] + p(1, 4)
    feed_start(1, mid_v[2])
    feed_both(1, acc, {1: lambda: begin(0)})
    begin(1)
    out_v[...] = acc[...].astype(BF16)
    acc[...], feed_small = feed_end(1, mid_v[2])
    mark()
    rows_start(1)

    def narrow_tail(l, rows):
        at = 2 * D + l * NARROW + NARROW - 16
        gd_v[at : at + 16, :] = small_rows(rows).astype(BF16)

    dc, dmem = mixture_bwd(
        acc[...].astype(BF16), low_v[1], mem_v[...], experts_of(xp_v, 2), xw, same_of(s_ends, t_ends), kept[1],
        gx_v, 0, gd_v, 2 * D + 2 * NARROW, mark,
    )
    cot_v[...] = dmem.astype(BF16)
    dbefore, dgain, dbias = norm_back(dc, mid_v[1], xp_v[0:1, :])
    narrow_tail(2, [dgain, dbias])
    mid_v[2] = acc[...] + dbefore
    begin(2)
    mark()

    def self_fwd(l):
        x = x_v[l].astype(F32)
        a = norm(x, p(l, 0), p(l, 1)).astype(BF16)
        low_v[0] = a
        at = 9 + 2 * sec
        experts = [laid_out(p_v[l, pl.ds(at + r, 1), :]) for r in range(2)]
        ends = t_ends if l else s_ends
        allowed = same_of(ends, ends)
        allowed = allowed & earlier() if l else allowed
        mixture_fwd(a, a, experts, weights(l, sm_v.at[l]), allowed, kept[0], False)

    def self_back(l, grad, wide, feed_small):
        at = 9 + 2 * sec
        experts = [laid_out(p_v[l, pl.ds(at + r, 1), :]) for r in range(2)]
        ends = t_ends if l else s_ends
        allowed = same_of(ends, ends)
        allowed = allowed & earlier() if l else allowed
        da, ds = mixture_bwd(
            grad[...].astype(BF16), low_v[0], low_v[0], experts, weights(l, sm_v.at[l]), allowed, kept[0],
            wide, 0, gd_v, 2 * D + l * NARROW, mark,
        )
        dx, dgain, dbias = norm_back(da + ds, x_v[l].astype(F32), p(l, 0))
        mid_v[l] = grad[...] + dx
        narrow_tail(l, [dgain, dbias] + feed_small + [deb[l, i : i + 1, :] for i in range(FF // D)])

    feed_start(0, mid_v[0])
    feed_both(0, None, {1: lambda: begin(3)})
    begin(4)
    acc[...], own_small = feed_end(0, mid_v[0])
    mark()
    swapped("wq", "wo", "x")
    self_fwd(0)
    mark()
    self_back(0, acc, ge_v, own_small)
    begin(5)
    mark()

    self_fwd(1)
    mark()
    self_back(1, mid_v.at[2], gd_v, feed_small)
    at = 2 * D + 3 * NARROW
    gd_v[at:, :] = jnp.zeros((2 * halves[6] - at, D), BF16)
    begin(6)
    gin_rows = gin_out.at[pl.ds(own_at, T)]
    gin_near = pltpu.make_async_copy(mid_v.at[sec], gin_rows, out_sem.at[13])
    gin_away = remote(mid_v.at[1 - sec], gin_rows, out_send.at[2], out_recv.at[2])
    gin_near.start()
    gin_away.start()
    mark()
    mark()
    while live:
        for k in list(live):
            advance(k)
    for wait in finals:
        wait()
    gin_near.wait()
    gin_away.wait()

    rows_end(0)
    rows_end(1)


def widen(act, gin, gff, gat, gx, *refs):
    outs, (act_v, gin_v, gff_v, gat_v, gx_v, ex_v, re_v, mats, in_sem, out_sem) = refs[:-10], refs[-10:]
    act_out, gin_out, expand, reduce, q, o, xq, xo = outs[:8]
    smalls = outs[8:]
    loads, at = [], 0
    for ref, dst in ((gff, gff_v), (gat, gat_v), (gx, gx_v)):
        for first in range(0, ref.shape[0], D):
            rows = pl.ds(first, min(D, ref.shape[0] - first))
            loads.append(pltpu.make_async_copy(ref.at[rows], dst.at[rows], in_sem.at[at]))
            loads[-1].start()
            at += 1
    passing = [
        pltpu.make_async_copy(a, b, in_sem.at[at + i]) for i, (a, b) in enumerate(((act, act_v), (gin, gin_v)))
    ]
    for copy in passing:
        copy.start()
    stores = []

    def store(src, dst):
        stores.append(pltpu.make_async_copy(src, dst, out_sem.at[len(stores)]))
        stores[-1].start()

    blocks = PART // D
    for i in range(2 * FF // D):
        loads[i].wait()
        part, kind, block = i // (2 * blocks), (i // blocks) % 2, i % blocks
        col = part * PART + block * D
        value = gff_v[i * D : (i + 1) * D, :].astype(F32)
        if kind == 0:
            ex_v[:, col : col + D] = value
            store(ex_v.at[:, pl.ds(col, D)], expand.at[:, pl.ds(col, D)])
        else:
            re_v[col : col + D, :] = value
            store(re_v.at[pl.ds(col, D)], reduce.at[pl.ds(col, D)])
    i = 2 * FF // D
    for m, (src, row, dst) in enumerate(((gat_v, 0, q), (gat_v, D, o), (gx_v, 0, xq), (gx_v, D, xo))):
        loads[i + m + m // 2].wait()
        mats[m] = src[row : row + D, :].astype(F32)
        store(mats.at[m], dst)
    for k, load in enumerate((loads[i + 2], loads[i + 5])):
        load.wait()
        src = (gat_v, gx_v)[k]
        ks, vs, rs = smalls[:3] if k == 0 else smalls[9:12]
        at = 2 * D
        ks[...] = src[at : at + 64, :].astype(F32)
        vs[...] = src[at + 64 : at + PAIR, :].astype(F32)
        rs[...] = src[at + PAIR : at + PAIR + 16, :].astype(F32)[0:8]
        tail = src[at + PAIR + 16 : at + NARROW, :].astype(F32)
        if k == 0:
            for j in range(5):
                smalls[3 + j][...] = tail[j : j + 1]
            for j in range(FF // D):
                smalls[8][:, j * D : (j + 1) * D] = tail[5 + j : 6 + j]
        else:
            for j in range(2):
                smalls[12 + j][...] = tail[j : j + 1]
    for copy, src, dst in zip(passing, (act_v, gin_v), (act_out, gin_out)):
        copy.wait()
        store(src, dst)
    for copy in stores:
        copy.wait()


def body(n, *arrays):
    (
        embeddings, cotangent, source_lengths, target_lengths, self_routes, cross_routes,
        attend_gain, attend_bias, self_router, query_weight, key_weight, value_weight, output_weight,
        feed_gain, feed_bias, expand_weight, expand_bias, reduce_weight, reduce_bias,
        cross_gain, cross_bias, cross_router, cross_query, cross_key, cross_value, cross_output,
    ) = arrays
    row_count = embeddings.shape[1]
    sents = source_lengths.shape[1]
    part = up(PART, n)
    halves = (part, part, up(D, n), part, part, up(D, n), up((2 * D + 3 * NARROW + 1) // 2, n))
    cut = [stream for i, half in enumerate(halves) for stream in streams_of(i, half, n)]
    streams, lands = len(cut), sum(stream[2] for stream in cut)
    steps = n.bit_length() - 1 + scattered(n) + 2
    S, V, DMA = jax.ShapeDtypeStruct, pltpu.VMEM, pltpu.SemaphoreType.DMA
    hbm, smem = pl.BlockSpec(memory_space=pl.ANY), pl.BlockSpec(memory_space=pltpu.SMEM)
    vmem = pl.BlockSpec(memory_space=pltpu.VMEM)
    rows = 2 * D + NARROW
    act, gin, gff, gat, gx = pl.pallas_call(
        functools.partial(fused, n, halves, sents),
        in_specs=[smem] * 2 + [vmem] * 16 + [hbm] * 8,
        out_specs=[hbm] * 5,
        out_shape=[
            S((row_count, D), BF16), S((row_count, D), F32),
            S((2 * FF, D), BF16), S((rows, D), BF16), S((rows, D), BF16),
        ],
        scratch_shapes=[
            V((3, T, D), BF16), V((2, 16, D), F32), V((16, D), F32), V((2, NARROW, D), BF16), V((NARROW, D), BF16),
            V((2, D, D), BF16), V((2, D, D), BF16), V((2, D, FF), BF16), V((2, FF, D), BF16),
            V((T, D), BF16), V((D, D), BF16), V((D, D), BF16),
            V((3, 3, PAIR, D), BF16), [[V(s, t) for _, s, t in KEPT] for _ in range(2)],
            V((2, T, D), BF16), V((3, T, D), F32), V((T, D), BF16), V((T, D), BF16), V((D, T), BF16),
            V((2, T, D), F32), V((2, 8, D), F32), V((T, D), BF16),
            V((2, PARTS, 2 * part, D), BF16), *(V((2 * halves[i], D), BF16) for i in (2, 5, 6)),
            V((2, max(halves), D), BF16), V((lands, D), BF16), DMA((streams,)), DMA((streams, steps)),
            pltpu.SemaphoreType.REGULAR((streams, 1 + scattered(n))),
            DMA((9,)), DMA((6 + 2 * FF // CH,)), DMA((6 + 2 * FF // CH,)), DMA((14,)), DMA((3,)), DMA((3,)),
        ],
        compiler_params=pltpu.CompilerParams(
            collective_id=0, has_side_effects=True, vmem_limit_bytes=(63 << 20) + (900 << 10)
        ),
    )(
        source_lengths, target_lengths, self_routes[0].T, cross_routes.T,
        attend_gain, attend_bias, feed_gain, feed_bias, reduce_bias, expand_bias,
        key_weight[0].T, value_weight[0].T, self_router[0].T,
        cross_gain[None], cross_bias[None], cross_key.T, cross_value.T, cross_router.T,
        embeddings[0], cotangent, query_weight[0], output_weight[0], expand_weight[0], reduce_weight[0],
        cross_query, cross_output,
    )
    wide = [(row_count, D), (row_count, D), (D, FF), (FF, D)] + [(D, D)] * 4
    narrow = [(64, D), (64, D), (8, D)] + [(1, D)] * 5 + [(1, FF)] + [(64, D), (64, D), (8, D)] + [(1, D)] * 2
    out = pl.pallas_call(
        widen,
        in_specs=[hbm] * 5,
        out_specs=[hbm] * len(wide) + [vmem] * len(narrow),
        out_shape=[S(s, BF16 if i == 0 else F32) for i, s in enumerate(wide + narrow)],
        scratch_shapes=[
            V((row_count, D), BF16), V((row_count, D), F32), V((2 * FF, D), BF16), V((rows, D), BF16), V((rows, D), BF16),
            V((D, FF), F32), V((FF, D), F32), V((4, D, D), F32), DMA((2 * FF // D + 8,)), DMA((2 * FF // D + 6,)),
        ],
        compiler_params=pltpu.CompilerParams(vmem_limit_bytes=(63 << 20) + (900 << 10)),
    )(act, gin, gff, gat, gx)
    act, gin, expand, reduce, q, o, xq, xo = out[:8]
    k, v, r, gains, biases, fgain, fbias, rbias, ebias, xk, xv, xr, xgain, xbias = out[8:]
    return (
        act[None], gin[None], gains, biases, r.T[None], q[None], k.T[None], v.T[None], o[None],
        fgain, fbias, expand[None], ebias, reduce[None], rbias,
        xgain[0], xbias[0], xr.T, xq, xk.T, xv.T, xo,
    )


def solution(mesh):
    n = mesh.shape["dp"]
    stacked, rows = P("section", None), P("dp", None)
    matrix, both = P("section", None, None), P("section", "dp", None)
    params = (
        stacked, stacked, matrix, matrix, matrix, matrix, matrix, stacked, stacked, matrix, stacked, matrix, stacked,
    ) + (P(),) * 7
    return jax.shard_map(
        functools.partial(body, n),
        mesh=mesh,
        in_specs=(both, rows, rows, rows, both, rows) + params,
        out_specs=(both, both) + params,
        check_vma=False,
    )
```

```python
import functools
import math

import jax
import jax.numpy as jnp
from jax import lax
from jax.experimental import pallas as pl
from jax.experimental.pallas import tpu as pltpu
from jax.sharding import PartitionSpec as P

EPSILON = 1e-05
SCORE_SCALE = 0.125
MASKED_SCORE = -1000000000.0
F32 = jnp.float32
BF16 = jnp.bfloat16
T = 512
D = 512
FF = 2048
PAIR = 128
CH = 512
PARTS = 2
PART = FF // PARTS
NARROW = 160
MESH = pl.DeviceIdType.MESH


def dot(a, b):
    return lax.dot_general(a, b, (((1,), (0,)), ((), ())), preferred_element_type=F32)


def dot_nt(a, b):
    return lax.dot_general(a, b, (((1,), (1,)), ((), ())), preferred_element_type=F32)


def dot_tn(a, b):
    return lax.dot_general(a, b, (((0,), (0,)), ((), ())), preferred_element_type=F32)


def iota(shape, axis):
    return lax.broadcasted_iota(jnp.int32, shape, axis)


def norm_parts(v):
    centred = v - jnp.mean(v, axis=-1, keepdims=True)
    spread = jnp.mean(centred * centred, axis=-1, keepdims=True)
    return centred, lax.rsqrt(spread + EPSILON)


def norm(v, gain, bias):
    centred, scale = norm_parts(v)
    return centred * scale * gain + bias


def norm_back(dn, v, gain):
    centred, scale = norm_parts(v)
    unit = centred * scale
    dgain = jnp.sum(dn * unit, axis=0, keepdims=True)
    dbias = jnp.sum(dn, axis=0, keepdims=True)
    dunit = dn * gain
    first = jnp.mean(dunit, axis=-1, keepdims=True)
    second = jnp.mean(dunit * unit, axis=-1, keepdims=True)
    return scale * (dunit - first - unit * second), dgain, dbias


def ids_of(ends, shape, axis):
    places = iota(shape, axis)
    total = jnp.zeros(shape, jnp.int32)
    for end in ends:
        total = total + (places >= end).astype(jnp.int32)
    return total


def ends_of(lengths):
    ends, total = [], jnp.int32(0)
    for length in lengths:
        total = total + length
        ends.append(total)
    return ends


def same_of(key_ends, query_ends):
    return ids_of(key_ends, (T, 1), 0) == ids_of(query_ends, (1, T), 1)


def earlier():
    return iota((T, T), 0) <= iota((T, T), 1)


def chosen(expert, block):
    return expert == (iota((T, PAIR), 1) // 64 + 2 * block).astype(F32)


def laid_out(row):
    return jnp.broadcast_to(row, (PAIR, T)).T


def mixture_fwd(a, s, experts, w, allowed, kept, with_out=True):
    wq, wk2, wv2, wkv, wr2, wo = w
    q = dot(a, wq[...])
    logits = dot_nt(a, wr2[...])
    kk = dot_nt(s, wk2[...]).astype(BF16)
    vv = dot_nt(s, wv2[...]).astype(BF16)
    kept["kk"][...] = kk
    kept["vv"][...] = vv
    lanes = iota((T, PAIR), 1).astype(F32)
    raised = [
        jnp.exp(jnp.sum(jnp.where(lanes == e, logits, 0.0), axis=-1, keepdims=True))
        for e in experts
    ]
    total = raised[0] + raised[1]
    gated = [jnp.zeros((T, PAIR), F32) for _ in range(4)]
    for r in range(2):
        gate = raised[r] / total
        kept["gate"][r] = jnp.broadcast_to(gate, (T, PAIR))
        qs = jnp.zeros((T, PAIR), F32)
        for b in range(4):
            qs = jnp.where(chosen(experts[r], b), q[:, b * PAIR : (b + 1) * PAIR], qs)
        qs = qs.astype(BF16)
        kept["qs"][r] = qs
        scores = jnp.where(allowed, dot_nt(kk, qs) * SCORE_SCALE, MASKED_SCORE)
        top = jnp.max(scores, axis=0, keepdims=True)
        p = jnp.exp(scores - top)
        inverse = 1.0 / jnp.sum(p, axis=0, keepdims=True)
        kept["top"][r : r + 1] = top
        kept["inv"][r : r + 1] = inverse
        chance = (p * inverse).astype(BF16)
        mixed = dot_tn(vv, chance).T
        kept["mixed"][r] = mixed
        weighted = gate * mixed
        for b in range(4):
            gated[b] = jnp.where(chosen(experts[r], b), weighted, gated[b])
    for b in range(4):
        kept["gated"][:, b * PAIR : (b + 1) * PAIR] = gated[b].astype(BF16)
    if with_out:
        return dot(kept["gated"][...], wo[...])


def mixture_bwd(dy, a, s, experts, w, allowed, kept, wide, base, narrow, nbase, mark):
    wq, wk2, wv2, wkv, wr2, wo = w
    wide[base + D : base + 2 * D, :] = dot_tn(kept["gated"][...], dy).astype(BF16)
    dgated = dot_nt(dy, wo[...]).astype(BF16).astype(F32)
    kk, vv = kept["kk"][...], kept["vv"][...]
    lanes = iota((T, PAIR), 1)
    dkk = jnp.zeros((T, PAIR), F32)
    dvv = jnp.zeros((T, PAIR), F32)
    dgates, gates, dqs = [], [], []
    for r in range(2):
        own = jnp.zeros((T, PAIR), F32)
        for b in range(4):
            own = jnp.where(chosen(experts[r], b), dgated[:, b * PAIR : (b + 1) * PAIR], own)
        gate = kept["gate"][r]
        gates.append(gate)
        dgates.append(jnp.sum(own * kept["mixed"][r], axis=-1, keepdims=True))
        dmixed = (gate * own).astype(BF16)
        qs = kept["qs"][r]
        scores = jnp.where(allowed, dot_nt(kk, qs) * SCORE_SCALE, MASKED_SCORE)
        p = jnp.exp(scores - kept["top"][r : r + 1]) * kept["inv"][r : r + 1]
        dp = dot_nt(vv, dmixed)
        both = jnp.sum(p * dp, axis=0, keepdims=True)
        ds = (p * (dp - both)).astype(BF16)
        dkk = dkk + dot(ds, qs)
        dvv = dvv + dot(p.astype(BF16), dmixed)
        dqs.append((dot_tn(kk, ds) * SCORE_SCALE).T)
        mark()
    dq = []
    for b in range(4):
        part = jnp.zeros((T, PAIR), F32)
        for r in range(2):
            part = jnp.where(chosen(experts[r], b), dqs[r], part)
        dq.append(part.astype(BF16))
    dq = jnp.concatenate(dq, axis=1)
    dk = (dkk + pltpu.roll(dkk, 64, 1)) * SCORE_SCALE
    dv = dvv + pltpu.roll(dvv, 64, 1)
    dkv = jnp.where(lanes < 64, dk, dv).astype(BF16)
    mean = gates[0] * dgates[0] + gates[1] * dgates[1]
    dl = jnp.zeros((T, PAIR), F32)
    for r in range(2):
        dl = jnp.where(((lanes % 8).astype(F32) == experts[r]) & (lanes < 16), gates[r] * (dgates[r] - mean), dl)
    high = dl.astype(BF16).astype(F32)
    dl = jnp.where(lanes < 8, high, dl - high).astype(BF16)
    wide[base : base + D, :] = dot_tn(a, dq).astype(BF16)
    narrow[nbase : nbase + PAIR, :] = dot_tn(dkv, s).astype(BF16)
    dwr = dot_tn(dl, a)
    dwr = dwr[0:8] + dwr[8:16]
    narrow[nbase + PAIR : nbase + PAIR + 16, :] = jnp.concatenate([dwr, jnp.zeros((8, D), F32)], axis=0).astype(BF16)
    da = dot_nt(dq, wq[...]) + dot(dl, wr2[...])
    ds = dot(dkv, wkv[...])
    return da, ds


C0, C1 = 0.7978845608028654, 0.044715


def gelu(pre):
    half = 0.5 * jnp.tanh(C0 * (pre + C1 * pre * pre * pre)) + 0.5
    return pre * half


def gelu_both(pre):
    square = pre * pre
    t = jnp.tanh(C0 * pre * (1.0 + C1 * square))
    half = 0.5 * t + 0.5
    slope = half + 0.5 * pre * (1.0 - t * t) * (C0 * (1.0 + 3.0 * C1 * square))
    return pre * half, slope


def expand_step(j, f, we, p):
    at = pl.multiple_of(j * CH, CH)
    return dot(f[...], we[:, pl.ds(at, CH)]) + p[pl.ds(5 + j, 1), :]


def feed_fwd(f, acc, we, p, wr, ready):
    def step(j, carry):
        ready(j)
        hidden = gelu(expand_step(j, f, we, p)).astype(BF16)
        acc[...] += dot(hidden, wr[pl.ds(pl.multiple_of(j * CH, CH), CH), :])
        return carry

    lax.fori_loop(0, FF // CH, step, 0)


def small_rows(rows, count=16):
    places = iota((count, D), 0)
    out = jnp.zeros((count, D), F32)
    for i, row in enumerate(rows):
        out = jnp.where(places == i, row, out)
    return out


KEPT = (
    ("kk", (T, PAIR), BF16),
    ("vv", (T, PAIR), BF16),
    ("gate", (2, T, PAIR), F32),
    ("qs", (2, T, PAIR), BF16),
    ("top", (8, T), F32),
    ("inv", (8, T), F32),
    ("mixed", (2, T, PAIR), F32),
    ("gated", (T, D), BF16),
)


class Here:
    def __init__(self, n):
        self.bits = n.bit_length() - 1
        self.sec = lax.axis_index("section")
        self.rank = lax.axis_index("dp")

    def side(self, b):
        return lax.rem(self.rank // (1 << b), 2)

    def partner(self, b):
        return (self.sec, self.rank + (1 - 2 * self.side(b)) * (1 << b))

    def twin(self):
        return (1 - self.sec, self.rank)


def scattered(n):
    return min(4, n.bit_length() - 1)


def up(rows, n):
    unit = 16 << scattered(n)
    return -(-rows // unit) * unit


PLAN = (
    ((1, (1, 0, 2, 3)), (2, (1, 0, 2, 3)), (1, (0, 1, 2, 3))),
    ((1, (2, 0, 1, 3)), (1, (0, 1, 2, 3)), (2, (0, 1, 2, 3))),
    ((1, (2, 1, 0, 3)), (1, (1, 2, 0, 3))),
    ((2, (2, 0, 1, 3)), (1, (1, 0, 2, 3)), (1, (1, 0, 2, 3))),
    ((1, (2, 0, 1, 3)), (1, (0, 1, 2, 3)), (2, (0, 1, 2, 3))),
    ((1, (1, 0, 2, 3)), (1, (2, 0, 1, 3))),
    ((1, (1, 0, 2, 3)), (1, (1, 0, 2, 3)), (1, (0, 1, 2, 3))),
)
MARKS = (
    (),
    (),
    (),
    (0, 2),
    (1, 3, 2, 4, 5, 6, 0, 7),
    (11, 12, 13),
    (9,),
    (1, 8, 10, 2, 3, 0, 4),
    (7, 12, 5),
    (11, 6, 3, 1, 2),
    (0, 4, 14, 15, 13, 12, 5, 9),
    (3,),
    (8, 1, 2, 10, 0, 7, 4, 11),
    (
        14, 6, 15, 12, 16, 17, 18, 13, 5, 9, 3, 8, 2, 11, 1, 10, 14, 0, 7, 15, 4, 6, 16, 12,
        13, 18, 5, 9, 17, 0, 1, 3, 8, 16, 11, 14, 2, 10, 15, 4, 7, 17, 6, 18, 12, 5, 13, 1,
        9, 0, 16, 3, 8, 4, 11, 17, 0, 14, 10, 18, 2, 15, 5, 12, 7, 6, 9, 13, 2, 16, 4, 3,
        17, 1, 4, 10, 14, 18, 8, 3, 15, 11, 7, 1, 12, 5, 13, 16, 6, 9, 14, 17, 15, 18, 5, 10,
        16, 7, 8, 6, 7, 11, 17, 13, 18, 6, 12, 9, 14, 12, 9, 15, 10, 8, 16, 18, 10, 17, 8, 11,
        14, 11, 15, 14, 16, 13, 15, 16, 17, 13, 18, 17, 18,
    ),
)


def streams_of(group, half, n):
    bits = n.bit_length() - 1
    shares = sum(share for share, _ in PLAN[group])
    out, at = [], 0
    for share, order in PLAN[group]:
        rows = half * share // shares
        piece = rows >> scattered(n)
        lands = rows - piece + (bits - scattered(n)) * piece
        out.append((at, rows, lands, [b for b in order if b < bits] + list(range(4, bits))))
        at += rows
    return out


def add_rows(dst, at, src, start, rows):
    block = math.gcd(rows, 128)

    def step(i, carry):
        to = pl.ds(pl.multiple_of(at + i * block, 16), block)
        dst[to, :] = dst[to, :] + src[pl.ds(pl.multiple_of(start + i * block, 16), block), :]
        return carry

    lax.fori_loop(0, rows // block, step, 0)


def sum_steps(here, g, twin_in, ring_in, send, recv, free, half, first, rows, order, owner):
    def remote(i, src, dst, device):
        return pltpu.make_async_remote_copy(
            src_ref=src, dst_ref=dst, send_sem=send, recv_sem=recv.at[i],
            device_id=device, device_id_type=MESH,
        )

    def rows_at(at, count):
        return g.at[pl.ds(pl.multiple_of(at, 16), count)]

    def signal(i, device):
        pl.semaphore_signal(free.at[i], inc=1, device_id=device, device_id_type=MESH)

    def summed(copy, credit, device, at, source, start, length):
        def end():
            copy.wait()
            if credit is not None:
                signal(credit, device)
            add_rows(g, at, source, start, length)

        return end

    def after(credit, copy):
        def start():
            pl.semaphore_wait(free.at[credit], 1)
            copy.start()

        return start

    mine = here.sec * half + first
    other = (1 - here.sec) * half + first
    copies = 0
    copy = remote(copies, rows_at(other, rows), twin_in.at[pl.ds(first, rows)], here.twin())
    moves = [(copy.start, summed(copy, 0, here.twin(), mine, twin_in, first, rows))]
    at, length, landing, trail = mine, rows, 0, []
    for step, b in enumerate(order):
        copies += 1
        partner = here.partner(b)
        if step >= 4:
            copy = remote(copies, rows_at(at, length), ring_in.at[pl.ds(landing, length)], partner)
            moves.append((copy.start, summed(copy, None, partner, at, ring_in, landing, length)))
            landing += length
            continue
        length //= 2
        side = here.side(b)
        keep, give = at + side * length, at + (1 - side) * length
        copy = remote(copies, rows_at(give, length), ring_in.at[pl.ds(landing, length)], partner)
        moves.append((copy.start, summed(copy, 1 + step, partner, keep, ring_in, landing, length)))
        trail.append((b, at, length))
        at, landing = keep, landing + length
    for step, (b, before, length) in reversed(list(enumerate(trail))):
        copies += 1
        copy = remote(copies, rows_at(at, length), rows_at(at, length), here.partner(b))
        moves.append((after(1 + step, copy), copy.wait))
        at = before
    copies += 1
    copy = remote(copies, rows_at(mine, rows), rows_at(mine, rows), here.twin())
    if owner is None:
        moves.append((after(0, copy), copy.wait))
    else:
        gives = here.sec != owner

        def start():
            pl.semaphore_wait(free.at[0], 1)
            pl.when(gives)(copy.start)

        def end():
            pl.when(gives)(copy.wait_send)
            pl.when(jnp.logical_not(gives))(copy.wait_recv)

        moves.append((start, end))
    ends = [end for _, end in moves]
    starts = [start for start, _ in moves[1:]]

    def both(end, start):
        def step():
            end()
            start()

        return step

    return [moves[0][0]] + [both(end, start) for end, start in zip(ends, starts)] + [ends[-1]]


def fused(n, halves, sents, *refs):
    (
        sl, tl, routes, xroutes, ag, ab, fg, fb, rb, eb, wk, wv, wrt, cg, cb, xwk, xwv, xwrt,
        emb, cot, wq, wo, we, wr, xwq, xwo,
        act_out, gin_out, gff_out, gat_out, gx_out,
        x_v, p_v, xp_v, sm_v, xsm_v, wq_v, wo_v, we_v, wr_v, cot_v, xwq_v, xwo_v,
        wsm, kept_refs, low_v, mid_v, mem_v, f_v, ft_v, totals, deb, out_v,
        gff, gx_v, ge_v, gd_v, twin_in, ring_in, sum_send, sum_recv, sum_free,
        own_sem, in_send, in_recv, out_sem, out_send, out_recv,
    ) = refs
    here = Here(n)
    sec = here.sec
    acc, dacc = totals.at[0], totals.at[1]
    barrier = pltpu.get_barrier_semaphore()
    pl.semaphore_signal(barrier, inc=1, device_id=here.twin(), device_id_type=MESH)
    for b in range(here.bits):
        pl.semaphore_signal(barrier, inc=1, device_id=here.partner(b), device_id_type=MESH)

    def slot(ref, which):
        return ref.at[pl.ds(pl.multiple_of(which * T, T), T)]

    def remote(src, dst, send, recv):
        return pltpu.make_async_remote_copy(
            src_ref=src, dst_ref=dst, send_sem=send, recv_sem=recv, device_id=here.twin(), device_id_type=MESH
        )

    local = {}
    for i, (name, src, dst) in enumerate((
        ("x_oth", slot(emb, 1 - sec), x_v.at[2]), ("x", slot(emb, sec), x_v.at[sec]), ("wq", wq, wq_v.at[sec]),
        ("wo", wo, wo_v.at[sec]), ("we", we, we_v.at[sec]), ("wr", wr, wr_v.at[sec]),
        ("xwq", xwq, xwq_v), ("xwo", xwo, xwo_v), ("cot", slot(cot, sec), cot_v),
    )):
        local[name] = pltpu.make_async_copy(src, dst, own_sem.at[i])
        local[name].start()

    def need(*names):
        for name in names:
            local[name].wait()

    own_at = pl.multiple_of(sec * T, T)
    p_v[sec] = small_rows(
        [ref[...] for ref in (ag, ab, fg, fb, rb)]
        + [eb[:, i * D : (i + 1) * D] for i in range(FF // D)]
        + [routes[r : r + 1, m * T : (m + 1) * T].astype(F32) for m in range(2) for r in range(2)]
    )
    xp_v[...] = small_rows(
        [cg[...], cb[...]] + [xroutes[r : r + 1, pl.ds(own_at, T)].astype(F32) for r in range(2)]
    )

    def pack(wk, wv, wrt):
        router = wrt[...].astype(F32)
        tail = jnp.concatenate([router, router, jnp.zeros((16, D), F32)], axis=0).astype(BF16)
        return jnp.concatenate([wk[...], wv[...], tail], axis=0)

    sm_v[sec] = pack(wk, wv, wrt)
    xsm_v[...] = pack(xwk, xwv, xwrt)

    def lay_small(l, ref):
        for i in range(2):
            half = ref[64 * i : 64 * i + 64]
            wsm[l, i] = jnp.concatenate([half, half], axis=0)
        wsm[l, 2] = jnp.concatenate([ref[128:144], jnp.zeros((112, D), BF16)], axis=0)

    def weights(l, small):
        return (
            wq_v.at[l], wsm.at[l, 0], wsm.at[l, 1], small.at[pl.ds(0, PAIR)], wsm.at[l, 2], wo_v.at[l],
        )

    def p(l, i):
        return p_v[l, i : i + 1, :]

    def experts_of(ref, first):
        return [laid_out(ref[first + r : first + r + 1, :]) for r in range(2)]

    kept = [dict(zip([k[0] for k in KEPT], k)) for k in kept_refs]

    lay_small(sec, sm_v.at[sec])

    def own_middle(i, carry):
        row = jnp.where(i == 0, 1 - sec, sec)
        ends = ends_of([jnp.where(sec == 0, sl[row, i], tl[row, i]) for i in range(sents)])
        allowed = same_of(ends, ends) & (earlier() | (sec == 0))
        x = x_v[jnp.where(i == 0, 2, sec)].astype(F32)
        a = norm(x, p(sec, 0), p(sec, 1)).astype(BF16)
        at = 9 + 2 * row
        experts = [laid_out(p_v[sec, pl.ds(at + r, 1), :]) for r in range(2)]
        totals[1 - i] = x + mixture_fwd(a, a, experts, weights(sec, sm_v.at[sec]), allowed, kept[0])

        @pl.when(i == 0)
        def _():
            pl.semaphore_wait(barrier, here.bits + 1)
            for name in ("middle", "p", "sm"):
                swaps[name].start()
            for j in range(FF // CH):
                for copy in feed_swaps(j):
                    copy.start()
            for name in ("wq", "wo", "x"):
                swaps[name].start()

        return carry

    swaps = {}
    for i, (name, src, dst) in enumerate((
        ("p", p_v.at[sec], p_v), ("sm", sm_v.at[sec], sm_v), ("wq", wq, wq_v), ("wo", wo, wo_v),
        ("x", slot(emb, 1 - sec), x_v), ("middle", dacc, mid_v),
    )):
        swaps[name] = remote(src, dst.at[sec], in_send.at[i], in_recv.at[i])

    def feed_swaps(j):
        rows = pl.ds(pl.multiple_of(j * CH, CH), CH)
        first = len(swaps) + 2 * j
        return (
            remote(we.at[:, rows], we_v.at[sec, :, rows], in_send.at[first], in_recv.at[first]),
            remote(wr.at[rows], wr_v.at[sec, rows], in_send.at[first + 1], in_recv.at[first + 1]),
        )

    def swapped(*names):
        for name in names:
            swaps[name].wait()

    need("x_oth", "x", "wq", "wo")
    lax.fori_loop(0, 2, own_middle, 0)
    need("we", "wr")
    mid_v[sec] = acc[...]
    swapped("middle", "p", "sm")
    f_v[...] = norm(mid_v[0], p(0, 2), p(0, 3)).astype(BF16)
    acc[...] = mid_v[0] + p(0, 4)

    def feed_ready(j):
        for copy in feed_swaps(j):
            copy.wait()

    feed_fwd(f_v, acc, we_v.at[0], p_v.at[0], wr_v.at[0], feed_ready)
    mem_v[...] = acc[...].astype(BF16)
    lay_small(1 - sec, sm_v.at[1 - sec])
    need("xwq", "xwo", "cot")
    lay_small(2, xsm_v)
    finals = []

    def hand_out(start, end):
        start()
        finals.append(end)

    own_rows = act_out.at[pl.ds(own_at, T)]
    rows_out = []
    for i, ref in enumerate((mem_v, out_v)):
        near = pltpu.make_async_copy(ref, own_rows, out_sem.at[i])
        away = remote(ref, own_rows, out_send.at[i], out_recv.at[i])
        rows_out.append((near, away))

    def rows_start(i):
        pl.when(sec == i)(rows_out[i][0].start)
        pl.when(sec != i)(rows_out[i][1].start)

    def rows_end(i):
        pl.when(sec != i)(rows_out[i][1].wait_send)

        @pl.when(sec == i)
        def _():
            rows_out[i][0].wait()
            rows_out[i][1].wait_recv()

    rows_start(0)

    s_ends, t_ends = (ends_of([ref[sec, i] for i in range(sents)]) for ref in (sl, tl))
    xw = (xwq_v, wsm.at[2, 0], wsm.at[2, 1], xsm_v.at[pl.ds(0, PAIR)], wsm.at[2, 2], xwo_v)
    c = norm(mid_v[1], xp_v[0:1, :], xp_v[1:2, :]).astype(BF16)
    low_v[1] = c
    mid_v[2] = mid_v[1] + mixture_fwd(c, mem_v[...], experts_of(xp_v, 2), xw, same_of(s_ends, t_ends), kept[1])

    groups = (
        (gff.at[1, 0], 1), (gff.at[1, 1], 1), (gx_v, None), (gff.at[0, 0], 0), (gff.at[0, 1], 0), (ge_v, 0), (gd_v, None),
    )
    live, waiting, state = {}, {}, {"stream": 0, "landed": 0, "mark": 0}
    steps_in_all = here.bits + scattered(n) + 3

    def done(i):
        pairs = {
            0: [(1, gff.at[1, 0], gff_out.at[pl.ds(0, FF)], 3)],
            1: [(1, gff.at[1, 1], gff_out.at[pl.ds(FF, FF)], 4)],
            2: [(None, gx_v, gx_out.at[pl.ds(0, 2 * D)], 5)],
            3: [(0, gff.at[0, 0], gff_out.at[pl.ds(0, FF)], 6)],
            4: [(0, gff.at[0, 1], gff_out.at[pl.ds(FF, FF)], 7)],
            5: [(0, ge_v, gat_out.at[pl.ds(0, 2 * D)], 8)],
            6: [(1, gd_v.at[pl.ds(0, 2 * D)], gat_out.at[pl.ds(0, 2 * D)], 9)]
            + [(l, gd_v.at[pl.ds(2 * D + l * NARROW, NARROW)], gat_out.at[pl.ds(2 * D, NARROW)], 10 + l) for l in range(2)]
            + [(None, gd_v.at[pl.ds(2 * D + 2 * NARROW, NARROW)], gx_out.at[pl.ds(2 * D, NARROW)], 12)],
        }
        for owner, src, dst, sem in pairs[i]:
            copy = pltpu.make_async_copy(src, dst, out_sem.at[sem])
            if owner is None:
                copy.start()
                finals.append(copy.wait)
            else:
                pl.when(sec == owner)(copy.start)
                finals.append(functools.partial(pl.when(sec == owner), copy.wait))

    def advance(k):
        i, steps = live[k]
        steps.pop(0)()
        if not steps:
            del live[k]
            if all(entry[0] != i for entry in live.values()):
                done(i)

    for i, (g, owner) in enumerate(groups):
        for first, rows, lands, order in streams_of(i, halves[i], n):
            k = state["stream"]
            steps = sum_steps(
                here, g, twin_in.at[i % 2], ring_in.at[pl.ds(state["landed"], lands)],
                sum_send.at[k], sum_recv.at[k], sum_free.at[k], halves[i], first, rows, order, owner,
            )
            waiting[k] = [i, steps]
            state["stream"] += 1
            state["landed"] += lands

    def begin(i):
        for k in [k for k in live if live[k][0] == i - 1 and len(live[k][1]) == steps_in_all - 1]:
            advance(k)
        for k in [k for k in waiting if waiting[k][0] == i]:
            live[k] = waiting.pop(k)
            advance(k)

    def mark():
        for k in MARKS[state["mark"]]:
            if k in live:
                advance(k)
        state["mark"] += 1

    def feed_start(l, middle):
        f = norm(middle, p(l, 2), p(l, 3))
        f_v[...] = f.astype(BF16)
        ft_v[...] = f.T.astype(BF16)
        dacc[...] = jnp.zeros_like(dacc)

    def feed_both(l, total, between):
        we, wr = we_v.at[l], wr_v.at[l]

        def step(j, carry):
            at = pl.multiple_of(j * CH, CH)
            part, to = lax.div(j, PART // CH), pl.multiple_of(lax.rem(j, PART // CH) * CH, CH)
            dy = cot_v[...]
            hidden, slope = gelu_both(expand_step(j, f_v, we, p_v.at[l]))
            hidden = hidden.astype(BF16)
            if total is not None:
                total[...] += dot(hidden, wr[pl.ds(at, CH), :])
            gff[l, part, pl.ds(pl.multiple_of(PART + to, CH), CH), :] = dot_tn(hidden, dy).astype(BF16)
            dpre = (dot_nt(dy, wr[pl.ds(at, CH), :]) * slope).astype(BF16)
            deb[l, pl.ds(j, 1), :] = jnp.sum(dpre.astype(F32), axis=0, keepdims=True)
            gff[l, part, pl.ds(to, CH), :] = dot(ft_v[...], dpre).astype(BF16)
            dacc[...] += dot_nt(dpre, we[:, pl.ds(at, CH)])
            for k, work in between.items():
                pl.when(j == k)(work)
            return carry

        lax.fori_loop(0, FF // CH, step, 0)

    def feed_end(l, middle):
        dend = cot_v[...].astype(F32)
        dmid, dgain, dbias = norm_back(dacc[...], middle, p(l, 2))
        return dmid + dend, [dgain, dbias, jnp.sum(dend, axis=0, keepdims=True)]

    acc[...] = mid_v[2] + p(1, 4)
    feed_start(1, mid_v[2])
    feed_both(1, acc, {1: lambda: begin(0)})
    begin(1)
    out_v[...] = acc[...].astype(BF16)
    acc[...], feed_small = feed_end(1, mid_v[2])
    mark()
    rows_start(1)

    def narrow_tail(l, rows):
        at = 2 * D + l * NARROW + NARROW - 16
        gd_v[at : at + 16, :] = small_rows(rows).astype(BF16)

    dc, dmem = mixture_bwd(
        acc[...].astype(BF16), low_v[1], mem_v[...], experts_of(xp_v, 2), xw, same_of(s_ends, t_ends), kept[1],
        gx_v, 0, gd_v, 2 * D + 2 * NARROW, mark,
    )
    cot_v[...] = dmem.astype(BF16)
    dbefore, dgain, dbias = norm_back(dc, mid_v[1], xp_v[0:1, :])
    narrow_tail(2, [dgain, dbias])
    mid_v[2] = acc[...] + dbefore
    begin(2)
    mark()

    def self_fwd(l):
        x = x_v[l].astype(F32)
        a = norm(x, p(l, 0), p(l, 1)).astype(BF16)
        low_v[0] = a
        at = 9 + 2 * sec
        experts = [laid_out(p_v[l, pl.ds(at + r, 1), :]) for r in range(2)]
        ends = t_ends if l else s_ends
        allowed = same_of(ends, ends)
        allowed = allowed & earlier() if l else allowed
        mixture_fwd(a, a, experts, weights(l, sm_v.at[l]), allowed, kept[0], False)

    def self_back(l, grad, wide, feed_small):
        at = 9 + 2 * sec
        experts = [laid_out(p_v[l, pl.ds(at + r, 1), :]) for r in range(2)]
        ends = t_ends if l else s_ends
        allowed = same_of(ends, ends)
        allowed = allowed & earlier() if l else allowed
        da, ds = mixture_bwd(
            grad[...].astype(BF16), low_v[0], low_v[0], experts, weights(l, sm_v.at[l]), allowed, kept[0],
            wide, 0, gd_v, 2 * D + l * NARROW, mark,
        )
        dx, dgain, dbias = norm_back(da + ds, x_v[l].astype(F32), p(l, 0))
        mid_v[l] = grad[...] + dx
        narrow_tail(l, [dgain, dbias] + feed_small + [deb[l, i : i + 1, :] for i in range(FF // D)])

    feed_start(0, mid_v[0])
    feed_both(0, None, {1: lambda: begin(3)})
    begin(4)
    acc[...], own_small = feed_end(0, mid_v[0])
    mark()
    swapped("wq", "wo", "x")
    self_fwd(0)
    mark()
    self_back(0, acc, ge_v, own_small)
    begin(5)
    mark()

    self_fwd(1)
    mark()
    self_back(1, mid_v.at[2], gd_v, feed_small)
    at = 2 * D + 3 * NARROW
    gd_v[at:, :] = jnp.zeros((2 * halves[6] - at, D), BF16)
    begin(6)
    gin_rows = gin_out.at[pl.ds(own_at, T)]
    gin_near = pltpu.make_async_copy(mid_v.at[sec], gin_rows, out_sem.at[13])
    gin_away = remote(mid_v.at[1 - sec], gin_rows, out_send.at[2], out_recv.at[2])
    gin_near.start()
    gin_away.start()
    mark()
    mark()
    while live:
        for k in list(live):
            advance(k)
    for wait in finals:
        wait()
    gin_near.wait()
    gin_away.wait()

    rows_end(0)
    rows_end(1)


def widen(act, gin, gff, gat, gx, *refs):
    outs, (act_v, gin_v, gff_v, gat_v, gx_v, ex_v, re_v, mats, in_sem, out_sem) = refs[:-10], refs[-10:]
    act_out, gin_out, expand, reduce, q, o, xq, xo = outs[:8]
    smalls = outs[8:]
    passing = [
        pltpu.make_async_copy(a, b, in_sem.at[i]) for i, (a, b) in enumerate(((act, act_v), (gin, gin_v)))
    ]
    for copy in passing:
        copy.start()
    loads, at = [], len(passing)
    for ref, dst in ((gff, gff_v), (gat, gat_v), (gx, gx_v)):
        for first in range(0, ref.shape[0], D):
            rows = pl.ds(first, min(D, ref.shape[0] - first))
            loads.append(pltpu.make_async_copy(ref.at[rows], dst.at[rows], in_sem.at[at]))
            loads[-1].start()
            at += 1
    stores = []

    def store(src, dst):
        stores.append(pltpu.make_async_copy(src, dst, out_sem.at[len(stores)]))
        stores[-1].start()

    for copy, src, dst in zip(passing, (act_v, gin_v), (act_out, gin_out)):
        copy.wait()
        store(src, dst)
    blocks = PART // D
    for i in range(2 * FF // D):
        loads[i].wait()
        part, kind, block = i // (2 * blocks), (i // blocks) % 2, i % blocks
        col = part * PART + block * D
        value = gff_v[i * D : (i + 1) * D, :].astype(F32)
        if kind == 0:
            ex_v[:, col : col + D] = value
            store(ex_v.at[:, pl.ds(col, D)], expand.at[:, pl.ds(col, D)])
        else:
            re_v[col : col + D, :] = value
            store(re_v.at[pl.ds(col, D)], reduce.at[pl.ds(col, D)])
    i = 2 * FF // D
    for m, (src, row, dst) in enumerate(((gat_v, 0, q), (gat_v, D, o), (gx_v, 0, xq), (gx_v, D, xo))):
        loads[i + m + m // 2].wait()
        mats[m] = src[row : row + D, :].astype(F32)
        store(mats.at[m], dst)
    for k, load in enumerate((loads[i + 2], loads[i + 5])):
        load.wait()
        src = (gat_v, gx_v)[k]
        ks, vs, rs = smalls[:3] if k == 0 else smalls[9:12]
        at = 2 * D
        ks[...] = src[at : at + 64, :].astype(F32)
        vs[...] = src[at + 64 : at + PAIR, :].astype(F32)
        rs[...] = src[at + PAIR : at + PAIR + 16, :].astype(F32)[0:8]
        tail = src[at + PAIR + 16 : at + NARROW, :].astype(F32)
        if k == 0:
            for j in range(5):
                smalls[3 + j][...] = tail[j : j + 1]
            for j in range(FF // D):
                smalls[8][:, j * D : (j + 1) * D] = tail[5 + j : 6 + j]
        else:
            for j in range(2):
                smalls[12 + j][...] = tail[j : j + 1]
    for copy in stores:
        copy.wait()


def body(n, *arrays):
    (
        embeddings, cotangent, source_lengths, target_lengths, self_routes, cross_routes,
        attend_gain, attend_bias, self_router, query_weight, key_weight, value_weight, output_weight,
        feed_gain, feed_bias, expand_weight, expand_bias, reduce_weight, reduce_bias,
        cross_gain, cross_bias, cross_router, cross_query, cross_key, cross_value, cross_output,
    ) = arrays
    row_count = embeddings.shape[1]
    sents = source_lengths.shape[1]
    part = up(PART, n)
    halves = (part, part, up(D, n), part, part, up(D, n), up((2 * D + 3 * NARROW + 1) // 2, n))
    cut = [stream for i, half in enumerate(halves) for stream in streams_of(i, half, n)]
    streams, lands = len(cut), sum(stream[2] for stream in cut)
    steps = n.bit_length() - 1 + scattered(n) + 2
    S, V, DMA = jax.ShapeDtypeStruct, pltpu.VMEM, pltpu.SemaphoreType.DMA
    hbm, smem = pl.BlockSpec(memory_space=pl.ANY), pl.BlockSpec(memory_space=pltpu.SMEM)
    vmem = pl.BlockSpec(memory_space=pltpu.VMEM)
    rows = 2 * D + NARROW
    act, gin, gff, gat, gx = pl.pallas_call(
        functools.partial(fused, n, halves, sents),
        in_specs=[smem] * 2 + [vmem] * 16 + [hbm] * 8,
        out_specs=[hbm] * 5,
        out_shape=[
            S((row_count, D), BF16), S((row_count, D), F32),
            S((2 * FF, D), BF16), S((rows, D), BF16), S((rows, D), BF16),
        ],
        scratch_shapes=[
            V((3, T, D), BF16), V((2, 16, D), F32), V((16, D), F32), V((2, NARROW, D), BF16), V((NARROW, D), BF16),
            V((2, D, D), BF16), V((2, D, D), BF16), V((2, D, FF), BF16), V((2, FF, D), BF16),
            V((T, D), BF16), V((D, D), BF16), V((D, D), BF16),
            V((3, 3, PAIR, D), BF16), [[V(s, t) for _, s, t in KEPT] for _ in range(2)],
            V((2, T, D), BF16), V((3, T, D), F32), V((T, D), BF16), V((T, D), BF16), V((D, T), BF16),
            V((2, T, D), F32), V((2, 8, D), F32), V((T, D), BF16),
            V((2, PARTS, 2 * part, D), BF16), *(V((2 * halves[i], D), BF16) for i in (2, 5, 6)),
            V((2, max(halves), D), BF16), V((lands, D), BF16), DMA((streams,)), DMA((streams, steps)),
            pltpu.SemaphoreType.REGULAR((streams, 1 + scattered(n))),
            DMA((9,)), DMA((6 + 2 * FF // CH,)), DMA((6 + 2 * FF // CH,)), DMA((14,)), DMA((3,)), DMA((3,)),
        ],
        compiler_params=pltpu.CompilerParams(
            collective_id=0, has_side_effects=True, vmem_limit_bytes=(63 << 20) + (900 << 10)
        ),
    )(
        source_lengths, target_lengths, self_routes[0].T, cross_routes.T,
        attend_gain, attend_bias, feed_gain, feed_bias, reduce_bias, expand_bias,
        key_weight[0].T, value_weight[0].T, self_router[0].T,
        cross_gain[None], cross_bias[None], cross_key.T, cross_value.T, cross_router.T,
        embeddings[0], cotangent, query_weight[0], output_weight[0], expand_weight[0], reduce_weight[0],
        cross_query, cross_output,
    )
    wide = [(row_count, D), (row_count, D), (D, FF), (FF, D)] + [(D, D)] * 4
    narrow = [(64, D), (64, D), (8, D)] + [(1, D)] * 5 + [(1, FF)] + [(64, D), (64, D), (8, D)] + [(1, D)] * 2
    out = pl.pallas_call(
        widen,
        in_specs=[hbm] * 5,
        out_specs=[hbm] * len(wide) + [vmem] * len(narrow),
        out_shape=[S(s, BF16 if i == 0 else F32) for i, s in enumerate(wide + narrow)],
        scratch_shapes=[
            V((row_count, D), BF16), V((row_count, D), F32), V((2 * FF, D), BF16), V((rows, D), BF16), V((rows, D), BF16),
            V((D, FF), F32), V((FF, D), F32), V((4, D, D), F32), DMA((2 * FF // D + 8,)), DMA((2 * FF // D + 6,)),
        ],
        compiler_params=pltpu.CompilerParams(vmem_limit_bytes=(63 << 20) + (900 << 10)),
    )(act, gin, gff, gat, gx)
    act, gin, expand, reduce, q, o, xq, xo = out[:8]
    k, v, r, gains, biases, fgain, fbias, rbias, ebias, xk, xv, xr, xgain, xbias = out[8:]
    return (
        act[None], gin[None], gains, biases, r.T[None], q[None], k.T[None], v.T[None], o[None],
        fgain, fbias, expand[None], ebias, reduce[None], rbias,
        xgain[0], xbias[0], xr.T, xq, xk.T, xv.T, xo,
    )


def solution(mesh):
    n = mesh.shape["dp"]
    stacked, rows = P("section", None), P("dp", None)
    matrix, both = P("section", None, None), P("section", "dp", None)
    params = (
        stacked, stacked, matrix, matrix, matrix, matrix, matrix, stacked, stacked, matrix, stacked, matrix, stacked,
    ) + (P(),) * 7
    return jax.shard_map(
        functools.partial(body, n),
        mesh=mesh,
        in_specs=(both, rows, rows, rows, both, rows) + params,
        out_specs=(both, both) + params,
        check_vma=False,
    )
```
